256 devices in a mesh: ctx: 32 (over x, z_hi, core), chan: 8 (over z_lo, y).
Axes of the slice: x: 4, y: 4, z: 8 (z_hi: 4, z_lo: 2; z = z_hi * 2 + z_lo), core: 2. Of those that a mesh axis runs over, the one named last changes fastest.
Arguments:
- loader_rows: bfloat16 [4096, 12288], P('ctx', 'chan'), parts along dimension 1, may hold values from -6 to 6
- row_pos: int32 [4096], P('ctx'), may hold values from 0 to 4095, as said below
- short_w: float32 [3, 12288], P(None, 'chan'), parts along dimension 1, may hold values from -3.5 to 3.5
- long_filter: float32 [4096, 4096], P('ctx', 'chan'), parts along dimension 1, may hold values from -4 to 4
- skip_gain: float32 [4096], P('chan'), parts along dimension 0, may hold values from -4 to 4
Outputs:
- gated_out: bfloat16 [4096, 4096], P('ctx', 'chan'), parts along dimension 1
The draws below stay inside these ranges and needn't reach their ends.
There are 8 independent parts, one for each index of `chan`. The reference program is written for one: setup_inputs(seed, part) draws one part's arguments, and reference() takes and returns one part's arrays. A program takes and returns all parts, laid end to end along the dimension named above; an argument that names none is the same for every part. Nothing has to cross between parts.
Inputs may be any that keep to these rules, and one draw needn't show every extreme that they name: row_pos names every position once; position p belongs to index p // 128 of ctx; the 128 rows of one index of ctx hold at most 8 positions of any one index, and exactly 8 in every draw.
All inputs are finite; a program needn't handle non-finite values.
Results may differ from the reference program's by a relative error of at most 0.001.
Values may be sent and summed in bfloat16 or wider, within the bound.
A program may use at most 64 MiB of HBM per device.

```python
import math
import jax
import jax.numpy as jnp

BUNDLE_WIDTH = 512
TOK_DEV = 128
KS = 3
TRACK_SPAN = 4096
SPECTRUM = 8192
MEAN_ROWS = 4
CAP = 8
N_CTX = 32


def draw_row_pos(key, part):
    sampler_seeds = jax.random.split(key, 4)
    half_count = N_CTX // 2
    firsts = jax.random.randint(sampler_seeds[0], (half_count,), 0, CAP + 1)
    firsts = firsts.at[0].set(CAP)
    pieces = jnp.concatenate([firsts, 2 * MEAN_ROWS - firsts])
    pieces = pieces[jax.random.permutation(sampler_seeds[1], N_CTX)]
    source = jnp.arange(N_CTX)[:, None]
    target = jnp.arange(N_CTX)[None, :]
    counts = pieces[(target - source) % N_CTX]
    rank_dst = jax.vmap(lambda single: jax.random.permutation(single, N_CTX))(jax.random.split(sampler_seeds[2], N_CTX)).T
    before_dst = rank_dst[:, None, :] < rank_dst[None, :, :]
    dst_start = jnp.sum(jnp.where(before_dst, counts[:, None, :], 0), axis=0)
    rank_src = jax.vmap(lambda single: jax.random.permutation(single, N_CTX))(jax.random.split(sampler_seeds[3], N_CTX))
    before_src = rank_src[:, :, None] < rank_src[:, None, :]
    src_start = jnp.sum(jnp.where(before_src, counts[:, :, None], 0), axis=1)
    offsets = jnp.arange(TOK_DEV)
    inside = (offsets[None, :, None] >= src_start[:, None, :]) & (offsets[None, :, None] < (src_start + counts)[:, None, :])
    position = target[None] * TOK_DEV + dst_start[:, None, :] + offsets[None, :, None] - src_start[:, None, :]
    result = jnp.sum(jnp.where(inside, position, 0), axis=2)
    return result.reshape(TRACK_SPAN).astype(jnp.int32)


def draw_long_filter(key, part):
    sampler_seeds = jax.random.split(key, 7)
    whole_count_lags = jnp.arange(TRACK_SPAN)[:, None]
    steps_float = whole_count_lags.astype(jnp.float32)
    slow_rate = jnp.exp(jax.random.uniform(sampler_seeds[0], (1, BUNDLE_WIDTH), minval=math.log(0.5 / TRACK_SPAN), maxval=math.log(2.0 / TRACK_SPAN)))
    fast_rate = jnp.exp(jax.random.uniform(sampler_seeds[5], (1, BUNDLE_WIDTH), minval=math.log(2.0 / TRACK_SPAN), maxval=math.log(1.0 / 30.0)))
    chooser = jax.random.uniform(sampler_seeds[6], (1, BUNDLE_WIDTH))
    rates = jnp.where(chooser < 0.5, slow_rate, fast_rate)
    rough = jax.random.truncated_normal(sampler_seeds[1], -4.0, 4.0, (TRACK_SPAN, BUNDLE_WIDTH))
    spike_location = jax.random.randint(sampler_seeds[2], (3, BUNDLE_WIDTH), 1, TRACK_SPAN)
    spike_retain_flags = jax.random.uniform(sampler_seeds[3], (3, BUNDLE_WIDTH), minval=0.5, maxval=0.8)
    fading_profile = jnp.exp(-rates * steps_float)
    for feature_slot in range(3):
        fading_profile = fading_profile * jnp.where(whole_count_lags >= spike_location[feature_slot][None, :], spike_retain_flags[feature_slot][None, :], 1.0)
    scale = jnp.sqrt(1.0 - jnp.exp(-2.0 * rates))
    return (fading_profile * scale * rough).astype(jnp.float32)


def level_of(own_key, shape, shards, least, largest):
    level, own = 1.0, jax.random.fold_in(own_key, 6)
    for dim, blocks in shards:
        steps = jnp.exp(jax.random.uniform(jax.random.fold_in(own, dim), (blocks,), jnp.float32, least / len(shards), largest / len(shards)))
        level = level * jnp.repeat(steps, shape[dim] // blocks).reshape([-1 if axis == dim else 1 for axis in range(len(shape))])
    return level


def normal_values(key, shape, spread, most, cuts=(), held_as=jnp.bfloat16):
    entries = spread * jax.random.normal(key, shape, jnp.float32)
    if cuts:
        entries = entries * level_of(key, shape, cuts, -0.22, 0.18)
    return jnp.clip(entries, -most, most).astype(held_as)


def setup_inputs(seed: int = 0, part: int = 0) -> dict:
    key_list = jax.random.split(jax.random.key(seed), 6)
    part_splits = jax.random.split(jax.random.fold_in(key_list[5], part), 6)
    loader_rows = normal_values(part_splits[0], (TRACK_SPAN, 3 * BUNDLE_WIDTH), 1.0, 6.0, ((0, 32),))
    row_pos = draw_row_pos(jax.random.fold_in(key_list[5], 71), part)
    short_w = normal_values(part_splits[2], (KS, 3 * BUNDLE_WIDTH), KS ** -0.5, 3.5, (), jnp.float32)
    long_filter = draw_long_filter(jax.random.fold_in(jax.random.fold_in(key_list[5], part), 71), part)
    skip_gain = normal_values(part_splits[4], (BUNDLE_WIDTH,), 1.0, 4.0, (), jnp.float32)
    return {"loader_rows": loader_rows, "row_pos": row_pos, "short_w": short_w, "long_filter": long_filter, "skip_gain": skip_gain}


def reference(loader_rows, row_pos, short_w, long_filter, skip_gain):
    seq_rows = jnp.zeros_like(loader_rows).at[row_pos].set(loader_rows)
    widened = seq_rows.astype(jnp.float32)
    padded = jnp.concatenate([jnp.zeros((KS - 1, widened.shape[1]), jnp.float32), widened], axis=0)
    featured = jnp.zeros_like(widened)
    for offset in range(KS):
        featured = featured + short_w[offset][None, :] * padded[KS - 1 - offset:KS - 1 - offset + TRACK_SPAN]
    q_feat = featured[:, :BUNDLE_WIDTH]
    k_feat = featured[:, BUNDLE_WIDTH:2 * BUNDLE_WIDTH]
    v_feat = featured[:, 2 * BUNDLE_WIDTH:]
    product = k_feat * v_feat
    spec_first = jnp.fft.rfft(product, n=SPECTRUM, axis=0)
    spec_second = jnp.fft.rfft(long_filter, n=SPECTRUM, axis=0)
    long_conv = jnp.fft.irfft(spec_first * spec_second, n=SPECTRUM, axis=0)[:TRACK_SPAN]
    return (q_feat * (long_conv + skip_gain[None, :] * product)).astype(jnp.bfloat16)
```

```python
import functools
import math

import jax
import jax.numpy as jnp
import ml_dtypes
import numpy as np
from jax import lax
from jax.experimental import pallas as pl
from jax.experimental.pallas import tpu as pltpu
from jax.sharding import PartitionSpec as P

N = 32
B = 128
C = 16
W = 512
CAP = 8
F32, BF16 = jnp.float32, jnp.bfloat16
NT = (((1,), (1,)), ((), ()))
TN = (((0,), (0,)), ((), ()))
NN = (((1,), (0,)), ((), ()))


def dot(a, b, dims=NN):
    return lax.dot_general(a, b, dims, preferred_element_type=F32)


def halves(x):
    hi = x.astype(BF16)
    return hi, (x - hi.astype(F32)).astype(BF16)


def np_halves(x):
    hi = x.astype(ml_dtypes.bfloat16)
    return hi, (x - hi.astype(np.float64)).astype(ml_dtypes.bfloat16)


@functools.cache
def tables():
    quarter = np.arange(N) + 0.25
    block = 2 * math.pi * np.outer(quarter, np.arange(N)) / N
    turn = 2 * math.pi * np.outer(quarter, np.arange(B)) / (N * B)
    lane = 2 * math.pi * (np.outer(np.arange(B), np.arange(B)) % B) / B
    hi, lo = np_halves(np.concatenate([np.cos(block), -np.sin(block)]))
    first = np.concatenate([hi, hi, lo], axis=1)
    hi, lo = np_halves(np.concatenate([np.cos(block.T), -np.sin(block.T)], axis=1) / (N * B))
    last = np.concatenate([hi, hi, lo], axis=1)
    twiddle = np.stack([np.cos(turn), np.sin(turn)]).astype(np.float32)
    c, s = np.cos(lane), np.sin(lane)
    fwd = np.stack(np_halves(np.block([[c, -s], [s, c]])))
    inv = np.stack(np_halves(np.block([[c, s], [-s, c]])))
    return first, twiddle, fwd, inv, last


def iota(shape, dim):
    return lax.broadcasted_iota(jnp.int32, shape, dim)


def wide(z, g_ref):
    hi, lo = halves(z)
    return dot(hi, g_ref[0]) + (dot(lo, g_ref[0]) + dot(hi, g_ref[1]))


def forward(src, first_ref, tw_ref, fwd_ref, dst):
    cos, sin = tw_ref[0], tw_ref[1]
    first = first_ref[...]
    for c in range(C):
        hi, lo = halves(src[pl.ds(c, N, C), :])
        y = dot(first, jnp.concatenate([hi, lo, hi], axis=0))
        re, im = y[:N], y[N:]
        dst[pl.ds(c * N, N), :] = jnp.concatenate(
            [re * cos + im * sin, im * cos - re * sin], axis=1
        )
    dst[...] = wide(dst[...], fwd_ref)


def kernel(
    rows_ref, pos_ref, w_ref, filt_ref, gain_ref, first_ref, tw_ref, fwd_ref, inv_ref, last_ref,
    out_ref,
    x_send, f_send, code_send, x_recv, f_recv, code_recv, onehot, place, cand,
    q_feat, prod, spec_p, spec_f, conv, o_send, o_recv,
    send_sems, recv_sems,
):
    me = lax.axis_index("ctx")
    barrier = pltpu.get_barrier_semaphore()

    def greet(k, _):
        pl.semaphore_signal(
            barrier,
            inc=1,
            device_id={"ctx": lax.rem(me + k, N)},
            device_id_type=pl.DeviceIdType.MESH,
        )
        return 0

    lax.fori_loop(1, N, greet, 0)

    pos = pos_ref[...]
    owner = pos // B
    across = jnp.broadcast_to(owner.astype(F32), (B, B))
    down = across.T
    earlier = (across == down) & (iota((B, B), 0) < iota((B, B), 1))
    rank = jnp.sum(jnp.where(earlier, 1.0, 0.0), axis=0, keepdims=True).astype(jnp.int32)
    code = (owner * CAP + rank) * B + (pos - owner * B)
    code_send[...] = code
    code_recv[me] = code

    per = B // C
    for part in range(3):
        for j in range(W // B):
            chunk = rows_ref[:, part * W + j * B : part * W + (j + 1) * B].T
            x_send[j * per : (j + 1) * per, part * C : (part + 1) * C, :] = chunk.reshape(per, C, B)
    for j in range(W // B):
        f_send[j * B : (j + 1) * B, :] = filt_ref[:, j * B : (j + 1) * B].T
    x_recv[me] = x_send[me]
    mine = pl.ds(pl.multiple_of(me * C, C), C)
    f_recv[mine, :] = f_send[mine, :]

    pl.semaphore_wait(barrier, N - 1)

    def copy(src, dst, i, to):
        return pltpu.make_async_remote_copy(
            src_ref=src,
            dst_ref=dst,
            send_sem=send_sems.at[i],
            recv_sem=recv_sems.at[i],
            device_id={"ctx": to},
            device_id_type=pl.DeviceIdType.MESH,
        )

    def send_code(k, _):
        copy(code_send, code_recv.at[me], 0, lax.rem(me + k, N)).start()
        return 0

    def send_rows(k, _):
        to = lax.rem(me + k, N)
        copy(x_send.at[to], x_recv.at[me], 1, to).start()
        return 0

    def send_filter(k, _):
        to = lax.rem(me + k, N)
        theirs = pl.ds(pl.multiple_of(to * C, C), C)
        copy(f_send.at[theirs, :], f_recv.at[mine, :], 2, to).start()
        return 0

    lax.fori_loop(1, N, send_code, 0)
    lax.fori_loop(1, N, send_rows, 0)
    lax.fori_loop(1, N, send_filter, 0)

    def arrived(buf, i, count):
        part = buf.at[pl.ds(0, count)]
        pltpu.make_async_copy(part, part, recv_sems.at[i]).wait()

    def left(buf, i, count):
        part = buf.at[pl.ds(0, count)]
        pltpu.make_async_copy(part, part, send_sems.at[i]).wait()

    pick = iota((C, W), 1) == me * C + iota((C, W), 0)

    def column(row):
        return jnp.sum(jnp.where(pick, row, 0.0), axis=1, keepdims=True)

    taps = [
        jnp.concatenate([column(w_ref[i : i + 1, p * W : (p + 1) * W]) for p in range(3)], axis=0)
        for i in range(3)
    ]
    gain = column(gain_ref[...])

    arrived(code_recv, 0, N - 1)

    def index(h, _):
        tiles = []
        for s in (2 * h, 2 * h + 1):
            code = code_recv[s]
            slot = code // B
            within = (code - slot * B + 1).astype(F32)
            hot = (iota((N * CAP, B), 0) == slot).astype(F32).astype(BF16)
            onehot[s] = hot
            at = dot(hot, jnp.broadcast_to(within, (B, B)).astype(BF16), NT)
            tile = (at == (iota((N * CAP, B), 1) + 1).astype(F32)).astype(F32)
            tiles.append(tile.reshape(N, CAP, B))
        both = jnp.concatenate(tiles, axis=1).astype(BF16)
        place[:, pl.ds(pl.multiple_of(h * 2 * CAP, 2 * CAP), 2 * CAP), :] = both
        return 0

    lax.fori_loop(0, N // 2, index, 0)

    arrived(x_recv, 1, N - 1)

    def spread(h, _):
        tiles = [
            dot(onehot[s], x_recv[s], NT).reshape(N, CAP, 3 * C) for s in (2 * h, 2 * h + 1)
        ]
        both = jnp.concatenate(tiles, axis=1).astype(BF16)
        cand[:, pl.ds(pl.multiple_of(h * 2 * CAP, 2 * CAP), 2 * CAP), :] = both
        return 0

    lax.fori_loop(0, N // 2, spread, 0)

    lane = iota((3 * C, B), 1)

    def block(o, before):
        seq = dot(cand[o], place[o], TN)
        feat = taps[0] * seq
        for i in (1, 2):
            moved = jnp.where(lane < i, pltpu.roll(before, i, 1), pltpu.roll(seq, i, 1))
            feat = feat + taps[i] * moved
        here = pl.ds(pl.multiple_of(o * C, C), C)
        q_feat[here, :] = feat[:C]
        prod[here, :] = feat[C : 2 * C] * feat[2 * C :]
        return seq

    lax.fori_loop(0, N, block, jnp.zeros((3 * C, B), F32))

    forward(prod, first_ref, tw_ref, fwd_ref, spec_p)
    arrived(f_recv, 2, (N - 1) * C)
    forward(f_recv, first_ref, tw_ref, fwd_ref, spec_f)

    a_re, a_im = spec_p[:, :B], spec_p[:, B:]
    b_re, b_im = spec_f[:, :B], spec_f[:, B:]
    z = jnp.concatenate([a_re * b_re - a_im * b_im, a_re * b_im + a_im * b_re], axis=1)
    spec_p[...] = wide(z, inv_ref)
    cos, sin = tw_ref[0], tw_ref[1]
    last = last_ref[...]
    for c in range(C):
        y = spec_p[pl.ds(c * N, N), :]
        re, im = y[:, :B], y[:, B:]
        hi, lo = halves(jnp.concatenate([re * cos - im * sin, im * cos + re * sin], axis=0))
        conv[pl.ds(c, N, C), :] = dot(last, jnp.concatenate([hi, lo, hi], axis=0))

    def finish(k, _):
        to = lax.rem(me + k, N)
        theirs = pl.ds(pl.multiple_of(to * C, C), C)
        value = q_feat[theirs, :] * (conv[theirs, :] + gain * prod[theirs, :])
        o_send[theirs, :] = value.astype(BF16)

        @pl.when(k < N)
        def _():
            copy(o_send.at[theirs, :], o_recv.at[mine, :], 3, to).start()

        return 0

    lax.fori_loop(1, N + 1, finish, 0)
    o_recv[mine, :] = o_send[mine, :]

    left(code_recv, 0, N - 1)
    left(x_send, 1, N - 1)
    left(f_send, 2, (N - 1) * C)
    left(o_send, 3, (N - 1) * C)
    arrived(o_recv, 3, (N - 1) * C)
    for j in range(W // B):
        out_ref[:, j * B : (j + 1) * B] = o_recv[j * B : (j + 1) * B, :].T


def body(loader_rows, row_pos, short_w, long_filter, skip_gain):
    consts = [jnp.asarray(t) for t in tables()]
    vmem = pl.BlockSpec(memory_space=pltpu.VMEM)
    return pl.pallas_call(
        kernel,
        out_shape=jax.ShapeDtypeStruct((B, W), BF16),
        in_specs=[vmem] * 10,
        out_specs=vmem,
        scratch_shapes=[
            pltpu.VMEM((N, 3 * C, B), BF16),
            pltpu.VMEM((W, B), F32),
            pltpu.VMEM((1, B), jnp.int32),
            pltpu.VMEM((N, 3 * C, B), BF16),
            pltpu.VMEM((W, B), F32),
            pltpu.VMEM((N, 1, B), jnp.int32),
            pltpu.VMEM((N, N * CAP, B), BF16),
            pltpu.VMEM((N, N * CAP, B), BF16),
            pltpu.VMEM((N, N * CAP, 3 * C), BF16),
            pltpu.VMEM((W, B), F32),
            pltpu.VMEM((W, B), F32),
            pltpu.VMEM((W, 2 * B), F32),
            pltpu.VMEM((W, 2 * B), F32),
            pltpu.VMEM((W, B), F32),
            pltpu.VMEM((W, B), BF16),
            pltpu.VMEM((W, B), BF16),
            pltpu.SemaphoreType.DMA((4,)),
            pltpu.SemaphoreType.DMA((4,)),
        ],
        compiler_params=pltpu.CompilerParams(
            collective_id=0, has_side_effects=True, vmem_limit_bytes=48 << 20
        ),
    )(loader_rows, row_pos.reshape(1, B), short_w, long_filter, skip_gain.reshape(1, W), *consts)


def solution(mesh):
    return jax.shard_map(
        body,
        mesh=mesh,
        in_specs=(P("ctx", "chan"), P("ctx"), P(None, "chan"), P("ctx", "chan"), P("chan")),
        out_specs=P("ctx", "chan"),
        check_vma=False,
    )
```

```python
import functools
import math

import jax
import jax.numpy as jnp
import ml_dtypes
import numpy as np
from jax import lax
from jax.experimental import pallas as pl
from jax.experimental.pallas import tpu as pltpu
from jax.sharding import PartitionSpec as P

N = 32
B = 128
C = 16
W = 512
ARGS = 10
CAP = 8
F32, BF16 = jnp.float32, jnp.bfloat16
NT = (((1,), (1,)), ((), ()))
TN = (((0,), (0,)), ((), ()))
NN = (((1,), (0,)), ((), ()))


def dot(a, b, dims=NN):
    return lax.dot_general(a, b, dims, preferred_element_type=F32)


def halves(x):
    hi = x.astype(BF16)
    return hi, (x - hi.astype(F32)).astype(BF16)


def np_halves(x):
    hi = x.astype(ml_dtypes.bfloat16)
    return hi, (x - hi.astype(np.float64)).astype(ml_dtypes.bfloat16)


@functools.cache
def tables():
    quarter = np.arange(N) + 0.25
    block = 2 * math.pi * np.outer(quarter, np.arange(N)) / N
    turn = 2 * math.pi * np.outer(quarter, np.arange(B)) / (N * B)
    lane = 2 * math.pi * (np.outer(np.arange(B), np.arange(B)) % B) / B
    hi, lo = np_halves(np.concatenate([np.cos(block), -np.sin(block)]))
    first = np.concatenate([hi, hi, lo], axis=1)
    hi, lo = np_halves(np.concatenate([np.cos(block.T), -np.sin(block.T)], axis=1) / (N * B))
    last = np.concatenate([hi, hi, lo], axis=1)
    twiddle = np.stack([np.cos(turn), np.sin(turn)]).astype(np.float32)
    c, s = np.cos(lane), np.sin(lane)
    fwd = np.stack(np_halves(np.block([[c, -s], [s, c]])))
    inv = np.stack(np_halves(np.block([[c, s], [-s, c]])))
    return first, twiddle, fwd, inv, last


def iota(shape, dim):
    return lax.broadcasted_iota(jnp.int32, shape, dim)


def wide(z, g_ref):
    hi, lo = halves(z)
    return dot(hi, g_ref[0]) + (dot(lo, g_ref[0]) + dot(hi, g_ref[1]))


def forward(src, first_ref, tw_ref, fwd_ref, dst):
    cos, sin = tw_ref[0], tw_ref[1]
    first = first_ref[...]
    for c in range(C):
        hi, lo = halves(src[pl.ds(c, N, C), :])
        y = dot(first, jnp.concatenate([hi, lo, hi], axis=0))
        re, im = y[:N], y[N:]
        dst[pl.ds(c * N, N), :] = jnp.concatenate(
            [re * cos + im * sin, im * cos - re * sin], axis=1
        )
    dst[...] = wide(dst[...], fwd_ref)


def kernel(
    *refs,
):
    given, out_ref, here = refs[:ARGS], refs[ARGS], refs[ARGS + 1 : 2 * ARGS + 1]
    scratch, load_sems = refs[2 * ARGS + 1 : -1], refs[-1]
    loads = [
        pltpu.make_async_copy(given[i], here[i], load_sems.at[i]) for i in range(ARGS)
    ]
    for load in loads:
        load.start()
    work(loads, *here, out_ref, *scratch)


def work(
    loads,
    pos_ref, rows_ref, filt_ref, w_ref, gain_ref, first_ref, tw_ref, last_ref, fwd_ref, inv_ref,
    out_ref,
    x_send, f_send, code_send, x_recv, f_recv, code_recv, onehot, place, cand,
    q_feat, prod, spec_p, spec_f, conv, o_send, o_recv,
    send_sems, recv_sems,
):
    me = lax.axis_index("ctx")
    barrier = pltpu.get_barrier_semaphore()

    def greet(k, _):
        pl.semaphore_signal(
            barrier,
            inc=1,
            device_id={"ctx": lax.rem(me + k, N)},
            device_id_type=pl.DeviceIdType.MESH,
        )
        return 0

    lax.fori_loop(1, N, greet, 0)

    loads[0].wait()
    pos = pos_ref[...]
    owner = pos // B
    across = jnp.broadcast_to(owner.astype(F32), (B, B))
    down = across.T
    earlier = (across == down) & (iota((B, B), 0) < iota((B, B), 1))
    rank = jnp.sum(jnp.where(earlier, 1.0, 0.0), axis=0, keepdims=True).astype(jnp.int32)
    code = (owner * CAP + rank) * B + (pos - owner * B)
    code_send[...] = code
    code_recv[me] = code

    loads[1].wait()
    per = B // C
    for part in range(3):
        for j in range(W // B):
            chunk = rows_ref[:, part * W + j * B : part * W + (j + 1) * B].T
            x_send[j * per : (j + 1) * per, part * C : (part + 1) * C, :] = chunk.reshape(per, C, B)
    loads[2].wait()
    for j in range(W // B):
        f_send[j * B : (j + 1) * B, :] = filt_ref[:, j * B : (j + 1) * B].T
    x_recv[me] = x_send[me]
    mine = pl.ds(pl.multiple_of(me * C, C), C)
    f_recv[mine, :] = f_send[mine, :]

    pl.semaphore_wait(barrier, N - 1)

    def copy(src, dst, i, to):
        return pltpu.make_async_remote_copy(
            src_ref=src,
            dst_ref=dst,
            send_sem=send_sems.at[i],
            recv_sem=recv_sems.at[i],
            device_id={"ctx": to},
            device_id_type=pl.DeviceIdType.MESH,
        )

    def send_code(k, _):
        copy(code_send, code_recv.at[me], 0, lax.rem(me + k, N)).start()
        return 0

    def send_rows(k, _):
        to = lax.rem(me + k, N)
        copy(x_send.at[to], x_recv.at[me], 1, to).start()
        return 0

    def send_filter(k, _):
        to = lax.rem(me + k, N)
        theirs = pl.ds(pl.multiple_of(to * C, C), C)
        copy(f_send.at[theirs, :], f_recv.at[mine, :], 2, to).start()
        return 0

    lax.fori_loop(1, N, send_code, 0)
    lax.fori_loop(1, N, send_rows, 0)
    lax.fori_loop(1, N, send_filter, 0)

    def arrived(buf, i, count):
        part = buf.at[pl.ds(0, count)]
        pltpu.make_async_copy(part, part, recv_sems.at[i]).wait()

    def left(buf, i, count):
        part = buf.at[pl.ds(0, count)]
        pltpu.make_async_copy(part, part, send_sems.at[i]).wait()

    for load in loads[3:]:
        load.wait()

    pick = iota((C, W), 1) == me * C + iota((C, W), 0)

    def column(row):
        return jnp.sum(jnp.where(pick, row, 0.0), axis=1, keepdims=True)

    taps = [
        jnp.concatenate([column(w_ref[i : i + 1, p * W : (p + 1) * W]) for p in range(3)], axis=0)
        for i in range(3)
    ]
    gain = column(gain_ref[...])

    arrived(code_recv, 0, N - 1)

    def index(h, _):
        tiles = []
        for s in (2 * h, 2 * h + 1):
            code = code_recv[s]
            slot = code // B
            within = (code - slot * B + 1).astype(F32)
            hot = (iota((N * CAP, B), 0) == slot).astype(F32).astype(BF16)
            onehot[s] = hot
            at = dot(hot, jnp.broadcast_to(within, (B, B)).astype(BF16), NT)
            tile = (at == (iota((N * CAP, B), 1) + 1).astype(F32)).astype(F32)
            tiles.append(tile.reshape(N, CAP, B))
        both = jnp.concatenate(tiles, axis=1).astype(BF16)
        place[:, pl.ds(pl.multiple_of(h * 2 * CAP, 2 * CAP), 2 * CAP), :] = both
        return 0

    lax.fori_loop(0, N // 2, index, 0)

    arrived(x_recv, 1, N - 1)

    def spread(h, _):
        tiles = [
            dot(onehot[s], x_recv[s], NT).reshape(N, CAP, 3 * C) for s in (2 * h, 2 * h + 1)
        ]
        both = jnp.concatenate(tiles, axis=1).astype(BF16)
        cand[:, pl.ds(pl.multiple_of(h * 2 * CAP, 2 * CAP), 2 * CAP), :] = both
        return 0

    lax.fori_loop(0, N // 2, spread, 0)

    lane = iota((3 * C, B), 1)

    def block(o, before):
        seq = dot(cand[o], place[o], TN)
        feat = taps[0] * seq
        for i in (1, 2):
            moved = jnp.where(lane < i, pltpu.roll(before, i, 1), pltpu.roll(seq, i, 1))
            feat = feat + taps[i] * moved
        here = pl.ds(pl.multiple_of(o * C, C), C)
        q_feat[here, :] = feat[:C]
        prod[here, :] = feat[C : 2 * C] * feat[2 * C :]
        return seq

    lax.fori_loop(0, N, block, jnp.zeros((3 * C, B), F32))

    forward(prod, first_ref, tw_ref, fwd_ref, spec_p)
    arrived(f_recv, 2, (N - 1) * C)
    forward(f_recv, first_ref, tw_ref, fwd_ref, spec_f)

    a_re, a_im = spec_p[:, :B], spec_p[:, B:]
    b_re, b_im = spec_f[:, :B], spec_f[:, B:]
    z = jnp.concatenate([a_re * b_re - a_im * b_im, a_re * b_im + a_im * b_re], axis=1)
    spec_p[...] = wide(z, inv_ref)
    cos, sin = tw_ref[0], tw_ref[1]
    last = last_ref[...]
    for c in range(C):
        y = spec_p[pl.ds(c * N, N), :]
        re, im = y[:, :B], y[:, B:]
        hi, lo = halves(jnp.concatenate([re * cos - im * sin, im * cos + re * sin], axis=0))
        conv[pl.ds(c, N, C), :] = dot(last, jnp.concatenate([hi, lo, hi], axis=0))

    def finish(k, _):
        to = lax.rem(me + k, N)
        theirs = pl.ds(pl.multiple_of(to * C, C), C)
        value = q_feat[theirs, :] * (conv[theirs, :] + gain * prod[theirs, :])
        o_send[theirs, :] = value.astype(BF16)

        @pl.when(k < N)
        def _():
            copy(o_send.at[theirs, :], o_recv.at[mine, :], 3, to).start()

        return 0

    lax.fori_loop(1, N + 1, finish, 0)
    o_recv[mine, :] = o_send[mine, :]

    left(code_recv, 0, N - 1)
    left(x_send, 1, N - 1)
    left(f_send, 2, (N - 1) * C)
    left(o_send, 3, (N - 1) * C)
    arrived(o_recv, 3, (N - 1) * C)
    for j in range(W // B):
        out_ref[:, j * B : (j + 1) * B] = o_recv[j * B : (j + 1) * B, :].T


def body(loader_rows, row_pos, short_w, long_filter, skip_gain):
    first, twiddle, fwd, inv, last = (jnp.asarray(t) for t in tables())
    operands = [
        row_pos.reshape(1, B), loader_rows, long_filter, short_w, skip_gain.reshape(1, W),
        first, twiddle, last, fwd, inv,
    ]
    return pl.pallas_call(
        kernel,
        out_shape=jax.ShapeDtypeStruct((B, W), BF16),
        in_specs=[pl.BlockSpec(memory_space=pltpu.HBM)] * ARGS,
        out_specs=pl.BlockSpec(memory_space=pltpu.VMEM),
        scratch_shapes=[
            *(pltpu.VMEM(x.shape, x.dtype) for x in operands),
            pltpu.VMEM((N, 3 * C, B), BF16),
            pltpu.VMEM((W, B), F32),
            pltpu.VMEM((1, B), jnp.int32),
            pltpu.VMEM((N, 3 * C, B), BF16),
            pltpu.VMEM((W, B), F32),
            pltpu.VMEM((N, 1, B), jnp.int32),
            pltpu.VMEM((N, N * CAP, B), BF16),
            pltpu.VMEM((N, N * CAP, B), BF16),
            pltpu.VMEM((N, N * CAP, 3 * C), BF16),
            pltpu.VMEM((W, B), F32),
            pltpu.VMEM((W, B), F32),
            pltpu.VMEM((W, 2 * B), F32),
            pltpu.VMEM((W, 2 * B), F32),
            pltpu.VMEM((W, B), F32),
            pltpu.VMEM((W, B), BF16),
            pltpu.VMEM((W, B), BF16),
            pltpu.SemaphoreType.DMA((4,)),
            pltpu.SemaphoreType.DMA((4,)),
            pltpu.SemaphoreType.DMA((ARGS,)),
        ],
        compiler_params=pltpu.CompilerParams(
            collective_id=0, has_side_effects=True, vmem_limit_bytes=60 << 20
        ),
    )(*operands)


def solution(mesh):
    return jax.shard_map(
        body,
        mesh=mesh,
        in_specs=(P("ctx", "chan"), P("ctx"), P(None, "chan"), P("ctx", "chan"), P("chan")),
        out_specs=P("ctx", "chan"),
        check_vma=False,
    )
```

```python
import functools
import math

import jax
import jax.numpy as jnp
import ml_dtypes
import numpy as np
from jax import lax
from jax.experimental import pallas as pl
from jax.experimental.pallas import tpu as pltpu
from jax.sharding import PartitionSpec as P

N = 32
B = 128
C = 16
W = 512
ARGS = 10
STEPS = 32767.0
CAP = 8
F32, BF16 = jnp.float32, jnp.bfloat16
NT = (((1,), (1,)), ((), ()))
TN = (((0,), (0,)), ((), ()))
NN = (((1,), (0,)), ((), ()))


def dot(a, b, dims=NN):
    return lax.dot_general(a, b, dims, preferred_element_type=F32)


def halves(x):
    hi = x.astype(BF16)
    return hi, (x - hi.astype(F32)).astype(BF16)


def np_halves(x):
    hi = x.astype(ml_dtypes.bfloat16)
    return hi, (x - hi.astype(np.float64)).astype(ml_dtypes.bfloat16)


@functools.cache
def tables():
    quarter = np.arange(N) + 0.25
    block = 2 * math.pi * np.outer(quarter, np.arange(N)) / N
    turn = 2 * math.pi * np.outer(quarter, np.arange(B)) / (N * B)
    lane = 2 * math.pi * (np.outer(np.arange(B), np.arange(B)) % B) / B
    hi, lo = np_halves(np.concatenate([np.cos(block), -np.sin(block)]))
    first = np.concatenate([hi, hi, lo], axis=1)
    hi, lo = np_halves(np.concatenate([np.cos(block.T), -np.sin(block.T)], axis=1) / (N * B))
    last = np.concatenate([hi, hi, lo], axis=1)
    twiddle = np.stack([np.cos(turn), np.sin(turn)]).astype(np.float32)
    c, s = np.cos(lane), np.sin(lane)
    fwd = np.stack(np_halves(np.block([[c, -s], [s, c]])))
    inv = np.stack(np_halves(np.block([[c, s], [-s, c]])))
    return first, twiddle, fwd, inv, last


def iota(shape, dim):
    return lax.broadcasted_iota(jnp.int32, shape, dim)


def wide(z, g_ref):
    hi, lo = halves(z)
    return dot(hi, g_ref[0]) + (dot(lo, g_ref[0]) + dot(hi, g_ref[1]))


def forward(src, gain, first_ref, tw_ref, fwd_ref, dst):
    cos, sin = tw_ref[0], tw_ref[1]
    first = first_ref[...]
    for c in range(C):
        x = src[pl.ds(c, N, C), :]
        if gain is not None:
            x = x * gain[:, c : c + 1]
        hi, lo = halves(x)
        y = dot(first, jnp.concatenate([hi, lo, hi], axis=0))
        re, im = y[:N], y[N:]
        dst[pl.ds(c * N, N), :] = jnp.concatenate(
            [re * cos + im * sin, im * cos - re * sin], axis=1
        )
    dst[...] = wide(dst[...], fwd_ref)


def kernel(
    *refs,
):
    given, out_ref, here = refs[:ARGS], refs[ARGS], refs[ARGS + 1 : 2 * ARGS + 1]
    scratch, load_sems = refs[2 * ARGS + 1 : -1], refs[-1]
    loads = [
        pltpu.make_async_copy(given[i], here[i], load_sems.at[i]) for i in range(ARGS)
    ]
    for load in loads:
        load.start()
    work(loads, *here, out_ref, *scratch)


def work(
    loads,
    pos_ref, rows_ref, filt_ref, w_ref, gain_ref, first_ref, tw_ref, last_ref, fwd_ref, inv_ref,
    out_ref,
    kv_send, q_send, f_send, note_send, kv_recv, q_recv, f_recv, note_recv,
    onehot, place, kv_cand, q_cand, prod, filt, spec_p, spec_f, conv, o_send, o_recv,
    send_sems, recv_sems, kv_sems, q_sems,
):
    me = lax.axis_index("ctx")
    barrier = pltpu.get_barrier_semaphore()

    def greet(k, _):
        pl.semaphore_signal(
            barrier,
            inc=1,
            device_id={"ctx": lax.rem(me + k, N)},
            device_id_type=pl.DeviceIdType.MESH,
        )
        return 0

    lax.fori_loop(1, N, greet, 0)

    loads[0].wait()
    pos = pos_ref[...]
    owner = pos // B
    across = jnp.broadcast_to(owner.astype(F32), (B, B))
    down = across.T
    earlier = (across == down) & (iota((B, B), 0) < iota((B, B), 1))
    rank = jnp.sum(jnp.where(earlier, 1.0, 0.0), axis=0, keepdims=True).astype(jnp.int32)
    code = ((owner * CAP + rank) * B + (pos - owner * B)).astype(F32)

    per = B // C

    def turned(part, j):
        return rows_ref[:, part * W + j * B : part * W + (j + 1) * B].T.reshape(per, C, B)

    loads[1].wait()
    for j in range(W // B):
        kv_send[j * per : (j + 1) * per, :C, :] = turned(1, j)
        kv_send[j * per : (j + 1) * per, C:, :] = turned(2, j)

    loads[2].wait()
    largest = jnp.maximum(jnp.max(jnp.abs(filt_ref[...]), axis=0, keepdims=True), 1e-33)
    unit = largest * (1.0 / STEPS)
    for j in range(W // B):
        note_send[j] = jnp.concatenate([code, unit[:, j * B : (j + 1) * B]], axis=0)
    mine = pl.ds(pl.multiple_of(me * C, C), C)
    note_recv[me] = note_send[me // per]

    pl.semaphore_wait(barrier, N - 1)

    def copy(src, dst, send_sem, recv_sem, to):
        return pltpu.make_async_remote_copy(
            src_ref=src,
            dst_ref=dst,
            send_sem=send_sem,
            recv_sem=recv_sem,
            device_id={"ctx": to},
            device_id_type=pl.DeviceIdType.MESH,
        )

    def send_note(k, _):
        to = lax.rem(me + k, N)
        copy(note_send.at[to // per], note_recv.at[me], send_sems.at[0], recv_sems.at[0], to).start()
        return 0

    def send_kv(k, _):
        to = lax.rem(me + k, N)
        copy(kv_send.at[to], kv_recv.at[k], send_sems.at[1], kv_sems.at[k], to).start()
        return 0

    def send_filter(k, _):
        to = lax.rem(me + k, N)
        theirs = pl.ds(pl.multiple_of(to * C, C), C)
        copy(f_send.at[theirs, :], f_recv.at[mine, :], send_sems.at[2], recv_sems.at[2], to).start()
        return 0

    def send_q(k, _):
        to = lax.rem(me + k, N)
        copy(q_send.at[to], q_recv.at[k], send_sems.at[3], q_sems.at[k], to).start()
        return 0

    lax.fori_loop(1, N, send_note, 0)
    lax.fori_loop(1, N, send_kv, 0)
    pltpu.make_async_copy(kv_send.at[me], kv_recv.at[0], kv_sems.at[0]).start()

    per_unit = STEPS / largest
    for j in range(W // B):
        part = slice(j * B, (j + 1) * B)
        steps = jnp.round(filt_ref[:, part] * per_unit[:, part]).T
        f_send[part, :] = steps.astype(jnp.int32).astype(jnp.int16)
    lax.fori_loop(1, N, send_filter, 0)
    f_recv[mine, :] = f_send[mine, :]

    for j in range(W // B):
        q_send[j * per : (j + 1) * per] = turned(0, j)
    lax.fori_loop(1, N, send_q, 0)
    pltpu.make_async_copy(q_send.at[me], q_recv.at[0], q_sems.at[0]).start()

    def arrived(part, sem):
        pltpu.make_async_copy(part, part, sem).wait()

    for load in loads[3:]:
        load.wait()

    pick = iota((C, W), 1) == me * C + iota((C, W), 0)

    def column(row):
        return jnp.sum(jnp.where(pick, row, 0.0), axis=1, keepdims=True)

    q_taps, k_taps, v_taps = (
        [column(w_ref[i : i + 1, p * W : (p + 1) * W]) for i in range(3)] for p in range(3)
    )
    kv_taps = [jnp.concatenate([k, v], axis=0) for k, v in zip(k_taps, v_taps)]
    gain = column(gain_ref[...])

    arrived(note_recv.at[pl.ds(0, N - 1)], recv_sems.at[0])

    def pair(h):
        return pl.ds(pl.multiple_of(h * 2 * CAP, 2 * CAP), 2 * CAP)

    def index(h, _):
        tiles = []
        for k in (2 * h, 2 * h + 1):
            code = note_recv[lax.rem(me - k + N, N)][:1].astype(jnp.int32)
            slot = code // B
            within = (code - slot * B + 1).astype(F32)
            hot = (iota((N * CAP, B), 0) == slot).astype(F32).astype(BF16)
            onehot[k] = hot
            at = dot(hot, jnp.broadcast_to(within, (B, B)).astype(BF16), NT)
            tile = (at == (iota((N * CAP, B), 1) + 1).astype(F32)).astype(F32)
            tiles.append(tile.reshape(N, CAP, B))
        place[:, pair(h), :] = jnp.concatenate(tiles, axis=1).astype(BF16)
        return 0

    lax.fori_loop(0, N // 2, index, 0, unroll=4)

    def spread(recv, sems, cand):
        def group(g, _):
            for i in range(8):
                k = g * 8 + i
                arrived(recv.at[k], sems.at[k])
            for i in range(4):
                h = g * 4 + i
                tiles = [
                    dot(onehot[k], recv[k], NT).reshape(N, CAP, recv.shape[1])
                    for k in (2 * h, 2 * h + 1)
                ]
                cand[:, pair(h), :] = jnp.concatenate(tiles, axis=1).astype(BF16)
            return 0

        lax.fori_loop(0, N // 8, group, 0)

    def filtered(taps, before, seq):
        lane = iota(seq.shape, 1)
        feat = taps[0] * seq
        for i in (1, 2):
            moved = jnp.where(lane < i, pltpu.roll(before, i, 1), pltpu.roll(seq, i, 1))
            feat = feat + taps[i] * moved
        return feat

    spread(kv_recv, kv_sems, kv_cand)

    def block(o, before):
        seq = dot(kv_cand[o], place[o], TN)
        feat = filtered(kv_taps, before, seq)
        prod[pl.ds(pl.multiple_of(o * C, C), C), :] = feat[:C] * feat[C:]
        return seq

    lax.fori_loop(0, N, block, jnp.zeros((2 * C, B), F32), unroll=8)

    forward(prod, None, first_ref, tw_ref, fwd_ref, spec_p)

    arrived(f_recv.at[pl.ds(0, (N - 1) * C)], recv_sems.at[2])
    filt[...] = f_recv[...].astype(jnp.int32).astype(F32)
    units = pltpu.roll(note_recv[:, 1, :], lax.rem(B - lax.rem(me, per) * C, B), 1)
    forward(filt, units, first_ref, tw_ref, fwd_ref, spec_f)

    a_re, a_im = spec_p[:, :B], spec_p[:, B:]
    b_re, b_im = spec_f[:, :B], spec_f[:, B:]
    z = jnp.concatenate([a_re * b_re - a_im * b_im, a_re * b_im + a_im * b_re], axis=1)
    spec_p[...] = wide(z, inv_ref)
    cos, sin = tw_ref[0], tw_ref[1]
    last = last_ref[...]
    for c in range(C):
        y = spec_p[pl.ds(c * N, N), :]
        re, im = y[:, :B], y[:, B:]
        hi, lo = halves(jnp.concatenate([re * cos - im * sin, im * cos + re * sin], axis=0))
        conv[pl.ds(c, N, C), :] = dot(last, jnp.concatenate([hi, lo, hi], axis=0))

    spread(q_recv, q_sems, q_cand)

    def finish(g, before):
        owners = [lax.rem(me + g * 8 + i + 1, N) for i in range(8)]
        parts = [pl.ds(pl.multiple_of(o * C, C), C) for o in owners]
        for o, theirs in zip(owners, parts):
            seq = dot(q_cand[o], place[o], TN)
            q_feat = filtered(q_taps, jnp.where(o == 0, 0.0, before), seq)
            value = q_feat * (conv[theirs, :] + gain * prod[theirs, :])
            o_send[theirs, :] = value.astype(BF16)
            before = seq

        def send(i):
            copy(o_send.at[parts[i], :], o_recv.at[mine, :], send_sems.at[4], recv_sems.at[4], owners[i]).start()

        for i in range(7):
            send(i)
        pl.when(g < N // 8 - 1)(lambda: send(7))
        return before

    lax.fori_loop(0, N // 8, finish, dot(q_cand[me], place[me], TN))
    o_recv[mine, :] = o_send[mine, :]

    most = pl.ds(0, (N - 1) * C)
    arrived(note_recv.at[pl.ds(0, N - 1)], send_sems.at[0])
    arrived(kv_send.at[pl.ds(0, N - 1)], send_sems.at[1])
    arrived(f_send.at[most], send_sems.at[2])
    arrived(q_send.at[pl.ds(0, N - 1)], send_sems.at[3])
    arrived(o_send.at[most], send_sems.at[4])
    arrived(o_recv.at[most], recv_sems.at[4])
    for j in range(W // B):
        out_ref[:, j * B : (j + 1) * B] = o_recv[j * B : (j + 1) * B, :].T


def body(loader_rows, row_pos, short_w, long_filter, skip_gain):
    first, twiddle, fwd, inv, last = (jnp.asarray(t) for t in tables())
    operands = [
        row_pos.reshape(1, B), loader_rows, long_filter, short_w, skip_gain.reshape(1, W),
        first, twiddle, last, fwd, inv,
    ]
    return pl.pallas_call(
        kernel,
        out_shape=jax.ShapeDtypeStruct((B, W), BF16),
        in_specs=[pl.BlockSpec(memory_space=pltpu.HBM)] * ARGS,
        out_specs=pl.BlockSpec(memory_space=pltpu.VMEM),
        scratch_shapes=[
            *(pltpu.VMEM(x.shape, x.dtype) for x in operands),
            pltpu.VMEM((N, 2 * C, B), BF16),
            pltpu.VMEM((N, C, B), BF16),
            pltpu.VMEM((W, B), jnp.int16),
            pltpu.VMEM((W // B, 2, B), F32),
            pltpu.VMEM((N, 2 * C, B), BF16),
            pltpu.VMEM((N, C, B), BF16),
            pltpu.VMEM((W, B), jnp.int16),
            pltpu.VMEM((N, 2, B), F32),
            pltpu.VMEM((N, N * CAP, B), BF16),
            pltpu.VMEM((N, N * CAP, B), BF16),
            pltpu.VMEM((N, N * CAP, 2 * C), BF16),
            pltpu.VMEM((N, N * CAP, C), BF16),
            pltpu.VMEM((W, B), F32),
            pltpu.VMEM((W, B), F32),
            pltpu.VMEM((W, 2 * B), F32),
            pltpu.VMEM((W, 2 * B), F32),
            pltpu.VMEM((W, B), F32),
            pltpu.VMEM((W, B), BF16),
            pltpu.VMEM((W, B), BF16),
            pltpu.SemaphoreType.DMA((5,)),
            pltpu.SemaphoreType.DMA((5,)),
            pltpu.SemaphoreType.DMA((N,)),
            pltpu.SemaphoreType.DMA((N,)),
            pltpu.SemaphoreType.DMA((ARGS,)),
        ],
        compiler_params=pltpu.CompilerParams(
            collective_id=0, has_side_effects=True, vmem_limit_bytes=60 << 20
        ),
    )(*operands)


def solution(mesh):
    return jax.shard_map(
        body,
        mesh=mesh,
        in_specs=(P("ctx", "chan"), P("ctx"), P(None, "chan"), P("ctx", "chan"), P("chan")),
        out_specs=P("ctx", "chan"),
        check_vma=False,
    )
```

```python
import functools
import math

import jax
import jax.numpy as jnp
import ml_dtypes
import numpy as np
from jax import lax
from jax.experimental import pallas as pl
from jax.experimental.pallas import tpu as pltpu
from jax.sharding import PartitionSpec as P

N = 32
B = 128
C = 16
W = 512
ARGS = 10
STEPS = 32767.0
CAP = 8
F32, BF16 = jnp.float32, jnp.bfloat16
NT = (((1,), (1,)), ((), ()))
TN = (((0,), (0,)), ((), ()))
NN = (((1,), (0,)), ((), ()))


def dot(a, b, dims=NN):
    return lax.dot_general(a, b, dims, preferred_element_type=F32)


def halves(x):
    hi = x.astype(BF16)
    return hi, (x - hi.astype(F32)).astype(BF16)


def np_halves(x):
    hi = x.astype(ml_dtypes.bfloat16)
    return hi, (x - hi.astype(np.float64)).astype(ml_dtypes.bfloat16)


@functools.cache
def tables():
    quarter = np.arange(N) + 0.25
    block = 2 * math.pi * np.outer(quarter, np.arange(N)) / N
    turn = 2 * math.pi * np.outer(quarter, np.arange(B)) / (N * B)
    lane = 2 * math.pi * (np.outer(np.arange(B), np.arange(B)) % B) / B
    hi, lo = np_halves(np.concatenate([np.cos(block), -np.sin(block)]))
    first = np.concatenate([hi, hi, lo], axis=1)
    hi, lo = np_halves(np.concatenate([np.cos(block.T), -np.sin(block.T)], axis=1) / (N * B))
    last = np.concatenate([hi, hi, lo], axis=1)
    twiddle = np.stack([np.cos(turn), np.sin(turn)]).astype(np.float32)
    c, s = np.cos(lane), np.sin(lane)
    fwd = np.stack(np_halves(np.block([[c, -s], [s, c]])))
    inv = np.stack(np_halves(np.block([[c, s], [-s, c]])))
    return first, twiddle, fwd, inv, last


def iota(shape, dim):
    return lax.broadcasted_iota(jnp.int32, shape, dim)


def wide(z, g_ref):
    hi, lo = halves(z)
    return dot(hi, g_ref[0]) + (dot(lo, g_ref[0]) + dot(hi, g_ref[1]))


def partner(me, step):
    a = step // 8
    return me ^ (jnp.where(a < 2, 2 + a, 3 - a) * 8 + 7 - step % 8)


def forward(src, gain, first_ref, tw_ref, fwd_ref, dst):
    cos, sin = tw_ref[0], tw_ref[1]
    first = first_ref[...]
    for c in range(C):
        x = src[pl.ds(c, N, C), :]
        if gain is not None:
            x = x * gain[:, c : c + 1]
        hi, lo = halves(x)
        y = dot(first, jnp.concatenate([hi, lo, hi], axis=0))
        re, im = y[:N], y[N:]
        dst[pl.ds(c * N, N), :] = jnp.concatenate(
            [re * cos + im * sin, im * cos - re * sin], axis=1
        )
    dst[...] = wide(dst[...], fwd_ref)


def kernel(
    *refs,
):
    given, out_ref, here = refs[:ARGS], refs[ARGS], refs[ARGS + 1 : 2 * ARGS + 1]
    scratch, load_sems = refs[2 * ARGS + 1 : -1], refs[-1]
    loads = [
        pltpu.make_async_copy(given[i], here[i], load_sems.at[i]) for i in range(ARGS)
    ]
    work(loads, *here, out_ref, *scratch)


def work(
    loads,
    pos_ref, rows_ref, filt_ref, w_ref, gain_ref, first_ref, tw_ref, last_ref, fwd_ref, inv_ref,
    out_ref,
    kv_send, q_send, f_send, note_send, kv_recv, q_recv, f_recv, note_recv,
    onehot, place, kv_cand, q_cand, q_feat, prod, filt, spec_p, spec_f, conv, o_send, o_recv,
    send_sems, recv_sems, kv_sems, q_sems,
):
    me = lax.axis_index("ctx")
    barrier = pltpu.get_barrier_semaphore()

    def greet(step, _):
        pl.semaphore_signal(
            barrier,
            inc=1,
            device_id={"ctx": partner(me, step)},
            device_id_type=pl.DeviceIdType.MESH,
        )
        return 0

    lax.fori_loop(0, N - 1, greet, 0)
    for load in loads:
        load.start()

    loads[0].wait()
    pos = pos_ref[...]
    owner = pos // B
    across = jnp.broadcast_to(owner.astype(F32), (B, B))
    down = across.T
    earlier = (across == down) & (iota((B, B), 0) < iota((B, B), 1))
    rank = jnp.sum(jnp.where(earlier, 1.0, 0.0), axis=0, keepdims=True).astype(jnp.int32)
    code = ((owner * CAP + rank) * B + (pos - owner * B)).astype(F32)

    per = B // C

    def turned(part, j):
        return rows_ref[:, part * W + j * B : part * W + (j + 1) * B].T.reshape(per, C, B)

    loads[1].wait()
    for j in range(W // B):
        kv_send[j * per : (j + 1) * per, :C, :] = turned(1, j)
        kv_send[j * per : (j + 1) * per, C:, :] = turned(2, j)

    loads[2].wait()
    largest = jnp.maximum(jnp.max(jnp.abs(filt_ref[...]), axis=0, keepdims=True), 1e-33)
    unit = largest * (1.0 / STEPS)
    for j in range(W // B):
        note_send[j] = jnp.concatenate([code, unit[:, j * B : (j + 1) * B]], axis=0)
    mine = pl.ds(pl.multiple_of(me * C, C), C)
    note_recv[me] = note_send[me // per]

    pl.semaphore_wait(barrier, N - 1)

    def copy(src, dst, send_sem, recv_sem, to):
        return pltpu.make_async_remote_copy(
            src_ref=src,
            dst_ref=dst,
            send_sem=send_sem,
            recv_sem=recv_sem,
            device_id={"ctx": to},
            device_id_type=pl.DeviceIdType.MESH,
        )

    def send_note(step, _):
        to = partner(me, step)
        copy(note_send.at[to // per], note_recv.at[me], send_sems.at[0], recv_sems.at[0], to).start()
        return 0

    def send_kv(step, _):
        to = partner(me, step)
        copy(kv_send.at[to], kv_recv.at[step], send_sems.at[1], kv_sems.at[step], to).start()
        return 0

    def send_q(step, _):
        to = partner(me, step)
        copy(q_send.at[to], q_recv.at[step], send_sems.at[3], q_sems.at[step], to).start()
        return 0

    def channels_of(to):
        return pl.ds(pl.multiple_of(to * C, C), C)

    def send_filter(step, _):
        to = partner(me, step)
        copy(f_send.at[channels_of(to), :], f_recv.at[mine, :], send_sems.at[2], recv_sems.at[2], to).start()
        return 0

    def send_out(step, _):
        to = partner(me, step)
        copy(o_send.at[channels_of(to), :], o_recv.at[mine, :], send_sems.at[4], recv_sems.at[4], to).start()
        return 0

    lax.fori_loop(0, N - 1, send_note, 0)
    lax.fori_loop(0, N - 1, send_kv, 0)
    pltpu.make_async_copy(kv_send.at[me], kv_recv.at[N - 1], kv_sems.at[N - 1]).start()

    for j in range(W // B):
        q_send[j * per : (j + 1) * per] = turned(0, j)
    lax.fori_loop(0, N - 1, send_q, 0)
    pltpu.make_async_copy(q_send.at[me], q_recv.at[N - 1], q_sems.at[N - 1]).start()

    per_unit = STEPS / largest
    for j in range(W // B):
        part = slice(j * B, (j + 1) * B)
        steps = jnp.round(filt_ref[:, part] * per_unit[:, part]).T
        f_send[part, :] = steps.astype(jnp.int32).astype(jnp.int16)
    lax.fori_loop(0, N - 1, send_filter, 0)
    f_recv[mine, :] = f_send[mine, :]

    def arrived(part, sem):
        pltpu.make_async_copy(part, part, sem).wait()

    for load in loads[3:]:
        load.wait()

    pick = iota((C, W), 1) == me * C + iota((C, W), 0)

    def column(row):
        return jnp.sum(jnp.where(pick, row, 0.0), axis=1, keepdims=True)

    q_taps, k_taps, v_taps = (
        [column(w_ref[i : i + 1, p * W : (p + 1) * W]) for i in range(3)] for p in range(3)
    )
    kv_taps = [jnp.concatenate([k, v], axis=0) for k, v in zip(k_taps, v_taps)]
    gain = column(gain_ref[...])

    arrived(note_recv.at[pl.ds(0, N - 1)], recv_sems.at[0])

    def pair(h):
        return pl.ds(pl.multiple_of(h * 2 * CAP, 2 * CAP), 2 * CAP)

    def index(h, _):
        tiles = []
        for k in (2 * h, 2 * h + 1):
            code = note_recv[partner(me, k)][:1].astype(jnp.int32)
            slot = code // B
            within = (code - slot * B + 1).astype(F32)
            hot = (iota((N * CAP, B), 0) == slot).astype(F32).astype(BF16)
            onehot[k] = hot
            at = dot(hot, jnp.broadcast_to(within, (B, B)).astype(BF16), NT)
            tile = (at == (iota((N * CAP, B), 1) + 1).astype(F32)).astype(F32)
            tiles.append(tile.reshape(N, CAP, B))
        place[:, pair(h), :] = jnp.concatenate(tiles, axis=1).astype(BF16)
        return 0

    lax.fori_loop(0, N // 2, index, 0, unroll=4)

    def spread(recv, sems, cand):
        def group(g, _):
            for i in range(8):
                k = g * 8 + i
                arrived(recv.at[k], sems.at[k])
            for i in range(4):
                h = g * 4 + i
                tiles = [
                    dot(onehot[k], recv[k], NT).reshape(N, CAP, recv.shape[1])
                    for k in (2 * h, 2 * h + 1)
                ]
                cand[:, pair(h), :] = jnp.concatenate(tiles, axis=1).astype(BF16)
            return 0

        lax.fori_loop(0, N // 8, group, 0)

    def filtered(taps, before, seq):
        lane = iota(seq.shape, 1)
        feat = taps[0] * seq
        for i in (1, 2):
            moved = jnp.where(lane < i, pltpu.roll(before, i, 1), pltpu.roll(seq, i, 1))
            feat = feat + taps[i] * moved
        return feat

    spread(kv_recv, kv_sems, kv_cand)

    def block(o, before):
        seq = dot(kv_cand[o], place[o], TN)
        feat = filtered(kv_taps, before, seq)
        prod[pl.ds(pl.multiple_of(o * C, C), C), :] = feat[:C] * feat[C:]
        return seq

    lax.fori_loop(0, N, block, jnp.zeros((2 * C, B), F32), unroll=8)

    forward(prod, None, first_ref, tw_ref, fwd_ref, spec_p)

    spread(q_recv, q_sems, q_cand)

    def q_block(o, before):
        seq = dot(q_cand[o], place[o], TN)
        q_feat[pl.ds(pl.multiple_of(o * C, C), C), :] = filtered(q_taps, before, seq)
        return seq

    lax.fori_loop(0, N, q_block, jnp.zeros((C, B), F32), unroll=8)

    arrived(f_recv.at[pl.ds(0, (N - 1) * C)], recv_sems.at[2])
    filt[...] = f_recv[...].astype(jnp.int32).astype(F32)
    units = pltpu.roll(note_recv[:, 1, :], lax.rem(B - lax.rem(me, per) * C, B), 1)
    forward(filt, units, first_ref, tw_ref, fwd_ref, spec_f)

    a_re, a_im = spec_p[:, :B], spec_p[:, B:]
    b_re, b_im = spec_f[:, :B], spec_f[:, B:]
    z = jnp.concatenate([a_re * b_re - a_im * b_im, a_re * b_im + a_im * b_re], axis=1)
    spec_p[...] = wide(z, inv_ref)
    cos, sin = tw_ref[0], tw_ref[1]
    last = last_ref[...]
    for c in range(C):
        y = spec_p[pl.ds(c * N, N), :]
        re, im = y[:, :B], y[:, B:]
        hi, lo = halves(jnp.concatenate([re * cos - im * sin, im * cos + re * sin], axis=0))
        conv[pl.ds(c, N, C), :] = dot(last, jnp.concatenate([hi, lo, hi], axis=0))

    def blocks(ref):
        return ref[...].reshape(N, C, B)

    gated = blocks(q_feat) * (blocks(conv) + gain[None] * blocks(prod))
    o_send[...] = gated.astype(BF16).reshape(W, B)
    lax.fori_loop(0, N - 1, send_out, 0)
    o_recv[mine, :] = o_send[mine, :]

    most = pl.ds(0, (N - 1) * C)
    arrived(o_recv.at[most], recv_sems.at[4])
    for j in range(W // B):
        out_ref[:, j * B : (j + 1) * B] = o_recv[j * B : (j + 1) * B, :].T
    arrived(note_recv.at[pl.ds(0, N - 1)], send_sems.at[0])
    arrived(kv_send.at[pl.ds(0, N - 1)], send_sems.at[1])
    arrived(f_send.at[most], send_sems.at[2])
    arrived(q_send.at[pl.ds(0, N - 1)], send_sems.at[3])
    arrived(o_send.at[most], send_sems.at[4])


def body(loader_rows, row_pos, short_w, long_filter, skip_gain):
    first, twiddle, fwd, inv, last = (jnp.asarray(t) for t in tables())
    operands = [
        row_pos.reshape(1, B), loader_rows, long_filter, short_w, skip_gain.reshape(1, W),
        first, twiddle, last, fwd, inv,
    ]
    return pl.pallas_call(
        kernel,
        out_shape=pltpu.VMEM((B, W), BF16),
        in_specs=[pl.BlockSpec(memory_space=pltpu.HBM)] * ARGS,
        out_specs=pl.BlockSpec(memory_space=pltpu.VMEM),
        scratch_shapes=[
            *(pltpu.VMEM(x.shape, x.dtype) for x in operands),
            pltpu.VMEM((N, 2 * C, B), BF16),
            pltpu.VMEM((N, C, B), BF16),
            pltpu.VMEM((W, B), jnp.int16),
            pltpu.VMEM((W // B, 2, B), F32),
            pltpu.VMEM((N, 2 * C, B), BF16),
            pltpu.VMEM((N, C, B), BF16),
            pltpu.VMEM((W, B), jnp.int16),
            pltpu.VMEM((N, 2, B), F32),
            pltpu.VMEM((N, N * CAP, B), BF16),
            pltpu.VMEM((N, N * CAP, B), BF16),
            pltpu.VMEM((N, N * CAP, 2 * C), BF16),
            pltpu.VMEM((N, N * CAP, C), BF16),
            pltpu.VMEM((W, B), F32),
            pltpu.VMEM((W, B), F32),
            pltpu.VMEM((W, B), F32),
            pltpu.VMEM((W, 2 * B), F32),
            pltpu.VMEM((W, 2 * B), F32),
            pltpu.VMEM((W, B), F32),
            pltpu.VMEM((W, B), BF16),
            pltpu.VMEM((W, B), BF16),
            pltpu.SemaphoreType.DMA((5,)),
            pltpu.SemaphoreType.DMA((5,)),
            pltpu.SemaphoreType.DMA((N,)),
            pltpu.SemaphoreType.DMA((N,)),
            pltpu.SemaphoreType.DMA((ARGS,)),
        ],
        compiler_params=pltpu.CompilerParams(
            collective_id=0, has_side_effects=True, vmem_limit_bytes=54 << 20
        ),
    )(*operands)


def solution(mesh):
    return jax.shard_map(
        body,
        mesh=mesh,
        in_specs=(P("ctx", "chan"), P("ctx"), P(None, "chan"), P("ctx", "chan"), P("chan")),
        out_specs=P("ctx", "chan"),
        check_vma=False,
    )
```

```python
import functools
import math

import jax
import jax.numpy as jnp
import ml_dtypes
import numpy as np
from jax import lax
from jax.experimental import pallas as pl
from jax.experimental.pallas import tpu as pltpu
from jax.sharding import PartitionSpec as P

N = 32
B = 128
C = 16
W = 512
ARGS = 10
LEVEL = 32768.0
STEPS = 32767.0
CAP = 8
F32, BF16 = jnp.float32, jnp.bfloat16
NT = (((1,), (1,)), ((), ()))
TN = (((0,), (0,)), ((), ()))
NN = (((1,), (0,)), ((), ()))


def dot(a, b, dims=NN):
    return lax.dot_general(a, b, dims, preferred_element_type=F32)


def unit_of(level):
    return jnp.exp2((level - 256.0) * 0.5)


def halves(x):
    hi = x.astype(BF16)
    return hi, (x - hi.astype(F32)).astype(BF16)


def np_halves(x):
    hi = x.astype(ml_dtypes.bfloat16)
    return hi, (x - hi.astype(np.float64)).astype(ml_dtypes.bfloat16)


@functools.cache
def tables():
    quarter = np.arange(N) + 0.25
    block = 2 * math.pi * np.outer(quarter, np.arange(N)) / N
    turn = 2 * math.pi * np.outer(quarter, np.arange(B)) / (N * B)
    lane = 2 * math.pi * (np.outer(np.arange(B), np.arange(B)) % B) / B
    hi, lo = np_halves(np.concatenate([np.cos(block), -np.sin(block)]))
    first = np.concatenate([hi, hi, lo], axis=1)
    hi, lo = np_halves(np.concatenate([np.cos(block.T), -np.sin(block.T)], axis=1) / (N * B))
    last = np.concatenate([hi, hi, lo], axis=1)
    twiddle = np.stack([np.cos(turn), np.sin(turn)]).astype(np.float32)
    c, s = np.cos(lane), np.sin(lane)
    fwd = np.stack(np_halves(np.block([[c, -s], [s, c]])))
    inv = np.stack(np_halves(np.block([[c, s], [-s, c]])))
    return first, twiddle, fwd, inv, last


def iota(shape, dim):
    return lax.broadcasted_iota(jnp.int32, shape, dim)


def wide(z, g_ref):
    hi, lo = halves(z)
    return dot(hi, g_ref[0]) + (dot(lo, g_ref[0]) + dot(hi, g_ref[1]))


def partner(me, step):
    a = step // 8
    return me ^ (jnp.where(a < 2, 2 + a, 3 - a) * 8 + 7 - step % 8)


def forward(src, gain, first_ref, tw_ref, fwd_ref, dst):
    cos, sin = tw_ref[0], tw_ref[1]
    first = first_ref[...]
    for c in range(C):
        x = src[pl.ds(c, N, C), :]
        if gain is not None:
            x = x * gain[:, c : c + 1]
        hi, lo = halves(x)
        y = dot(first, jnp.concatenate([hi, lo, hi], axis=0))
        re, im = y[:N], y[N:]
        dst[pl.ds(c * N, N), :] = jnp.concatenate(
            [re * cos + im * sin, im * cos - re * sin], axis=1
        )
    dst[...] = wide(dst[...], fwd_ref)


def kernel(
    *refs,
):
    given, out_ref, here = refs[:ARGS], refs[ARGS], refs[ARGS + 1 : 2 * ARGS + 1]
    scratch, load_sems = refs[2 * ARGS + 1 : -1], refs[-1]
    loads = [
        pltpu.make_async_copy(given[i], here[i], load_sems.at[i]) for i in range(ARGS)
    ]
    work(loads, *here, out_ref, *scratch)


def work(
    loads,
    pos_ref, rows_ref, filt_ref, w_ref, gain_ref, first_ref, tw_ref, last_ref, fwd_ref, inv_ref,
    out_ref,
    kv_send, q_send, f_send, note_send, kv_recv, q_recv, f_recv, note_recv,
    onehot, place, kv_cand, q_cand, q_feat, prod, filt, spec_p, spec_f, conv, o_send, o_recv,
    send_sems, recv_sems, kv_sems, q_sems,
):
    me = lax.axis_index("ctx")
    barrier = pltpu.get_barrier_semaphore()

    def greet(step, _):
        pl.semaphore_signal(
            barrier,
            inc=1,
            device_id={"ctx": partner(me, step)},
            device_id_type=pl.DeviceIdType.MESH,
        )
        return 0

    lax.fori_loop(0, N - 1, greet, 0)
    for load in loads:
        load.start()

    loads[0].wait()
    pos = pos_ref[...]
    owner = pos // B
    across = jnp.broadcast_to(owner.astype(F32), (B, B))
    down = across.T
    earlier = (across == down) & (iota((B, B), 0) < iota((B, B), 1))
    rank = jnp.sum(jnp.where(earlier, 1.0, 0.0), axis=0, keepdims=True).astype(jnp.int32)
    code = ((owner * CAP + rank) * B + (pos - owner * B)).astype(F32)

    per = B // C

    def turned(part, j):
        return rows_ref[:, part * W + j * B : part * W + (j + 1) * B].T.reshape(per, C, B)

    loads[1].wait()
    for j in range(W // B):
        kv_send[j * per : (j + 1) * per, :C, :] = turned(1, j)
        kv_send[j * per : (j + 1) * per, C:, :] = turned(2, j)

    loads[2].wait()
    largest = jnp.maximum(jnp.max(jnp.abs(filt_ref[...]), axis=0, keepdims=True), 1e-33)
    level = jnp.clip(jnp.ceil(2.0 * jnp.log2(largest * (1.0 / STEPS))) + 256.0, 1.0, 254.0)
    level = jnp.where(unit_of(level) * STEPS < largest, level + 1.0, level)
    for j in range(W // B):
        note_send[j] = level[:, j * B : (j + 1) * B] * LEVEL + code
    mine = pl.ds(pl.multiple_of(me * C, C), C)
    note_recv[me] = note_send[me // per]

    pl.semaphore_wait(barrier, N - 1)

    def copy(src, dst, send_sem, recv_sem, to):
        return pltpu.make_async_remote_copy(
            src_ref=src,
            dst_ref=dst,
            send_sem=send_sem,
            recv_sem=recv_sem,
            device_id={"ctx": to},
            device_id_type=pl.DeviceIdType.MESH,
        )

    def send_note(step, _):
        to = partner(me, step)
        copy(note_send.at[to // per], note_recv.at[me], send_sems.at[0], recv_sems.at[0], to).start()
        return 0

    def send_kv(step, _):
        to = partner(me, step)
        copy(kv_send.at[to], kv_recv.at[step], send_sems.at[1], kv_sems.at[step], to).start()
        return 0

    def send_q(step, _):
        to = partner(me, step)
        copy(q_send.at[to], q_recv.at[step], send_sems.at[3], q_sems.at[step], to).start()
        return 0

    def channels_of(to):
        return pl.ds(pl.multiple_of(to * C, C), C)

    def send_filter(step, _):
        to = partner(me, step)
        copy(f_send.at[channels_of(to), :], f_recv.at[mine, :], send_sems.at[2], recv_sems.at[2], to).start()
        return 0

    def send_out(step, _):
        to = partner(me, step)
        copy(o_send.at[channels_of(to), :], o_recv.at[mine, :], send_sems.at[4], recv_sems.at[4], to).start()
        return 0

    lax.fori_loop(0, N - 1, send_note, 0)
    lax.fori_loop(0, N - 1, send_kv, 0)
    pltpu.make_async_copy(kv_send.at[me], kv_recv.at[N - 1], kv_sems.at[N - 1]).start()

    for j in range(W // B):
        q_send[j * per : (j + 1) * per] = turned(0, j)
    lax.fori_loop(0, N - 1, send_q, 0)
    pltpu.make_async_copy(q_send.at[me], q_recv.at[N - 1], q_sems.at[N - 1]).start()

    per_unit = 1.0 / unit_of(level)
    for j in range(W // B):
        part = slice(j * B, (j + 1) * B)
        steps = jnp.round(filt_ref[:, part] * per_unit[:, part]).T
        f_send[part, :] = steps.astype(jnp.int32).astype(jnp.int16)
    lax.fori_loop(0, N - 1, send_filter, 0)
    f_recv[mine, :] = f_send[mine, :]

    def arrived(part, sem):
        pltpu.make_async_copy(part, part, sem).wait()

    for load in loads[3:]:
        load.wait()

    pick = iota((C, W), 1) == me * C + iota((C, W), 0)

    def column(row):
        return jnp.sum(jnp.where(pick, row, 0.0), axis=1, keepdims=True)

    q_taps, k_taps, v_taps = (
        [column(w_ref[i : i + 1, p * W : (p + 1) * W]) for i in range(3)] for p in range(3)
    )
    kv_taps = [jnp.concatenate([k, v], axis=0) for k, v in zip(k_taps, v_taps)]
    gain = column(gain_ref[...])

    arrived(note_recv.at[pl.ds(0, N - 1)], recv_sems.at[0])

    def pair(h):
        return pl.ds(pl.multiple_of(h * 2 * CAP, 2 * CAP), 2 * CAP)

    def index(h, _):
        tiles = []
        for k in (2 * h, 2 * h + 1):
            note = note_recv[partner(me, k)]
            code = (note - jnp.floor(note * (1.0 / LEVEL)) * LEVEL).astype(jnp.int32)
            slot = code // B
            within = (code - slot * B + 1).astype(F32)
            hot = (iota((N * CAP, B), 0) == slot).astype(F32).astype(BF16)
            onehot[k] = hot
            at = dot(hot, jnp.broadcast_to(within, (B, B)).astype(BF16), NT)
            tile = (at == (iota((N * CAP, B), 1) + 1).astype(F32)).astype(F32)
            tiles.append(tile.reshape(N, CAP, B))
        place[:, pair(h), :] = jnp.concatenate(tiles, axis=1).astype(BF16)
        return 0

    lax.fori_loop(0, N // 2, index, 0, unroll=4)

    def spread(recv, sems, cand):
        def group(g, _):
            for i in range(8):
                k = g * 8 + i
                arrived(recv.at[k], sems.at[k])
            for i in range(4):
                h = g * 4 + i
                tiles = [
                    dot(onehot[k], recv[k], NT).reshape(N, CAP, recv.shape[1])
                    for k in (2 * h, 2 * h + 1)
                ]
                cand[:, pair(h), :] = jnp.concatenate(tiles, axis=1).astype(BF16)
            return 0

        lax.fori_loop(0, N // 8, group, 0)

    def filtered(taps, before, seq):
        lane = iota(seq.shape, 1)
        feat = taps[0] * seq
        for i in (1, 2):
            moved = jnp.where(lane < i, pltpu.roll(before, i, 1), pltpu.roll(seq, i, 1))
            feat = feat + taps[i] * moved
        return feat

    spread(kv_recv, kv_sems, kv_cand)

    def block(o, before):
        seq = dot(kv_cand[o], place[o], TN)
        feat = filtered(kv_taps, before, seq)
        prod[pl.ds(pl.multiple_of(o * C, C), C), :] = feat[:C] * feat[C:]
        return seq

    lax.fori_loop(0, N, block, jnp.zeros((2 * C, B), F32), unroll=8)

    forward(prod, None, first_ref, tw_ref, fwd_ref, spec_p)

    spread(q_recv, q_sems, q_cand)

    def q_block(o, before):
        seq = dot(q_cand[o], place[o], TN)
        q_feat[pl.ds(pl.multiple_of(o * C, C), C), :] = filtered(q_taps, before, seq)
        return seq

    lax.fori_loop(0, N, q_block, jnp.zeros((C, B), F32), unroll=8)

    arrived(f_recv.at[pl.ds(0, (N - 1) * C)], recv_sems.at[2])
    filt[...] = f_recv[...].astype(jnp.int32).astype(F32)
    units = unit_of(jnp.floor(note_recv[:, 0, :] * (1.0 / LEVEL)))
    units = pltpu.roll(units, lax.rem(B - lax.rem(me, per) * C, B), 1)
    forward(filt, units, first_ref, tw_ref, fwd_ref, spec_f)

    a_re, a_im = spec_p[:, :B], spec_p[:, B:]
    b_re, b_im = spec_f[:, :B], spec_f[:, B:]
    z = jnp.concatenate([a_re * b_re - a_im * b_im, a_re * b_im + a_im * b_re], axis=1)
    spec_p[...] = wide(z, inv_ref)
    cos, sin = tw_ref[0], tw_ref[1]
    last = last_ref[...]
    for c in range(C):
        y = spec_p[pl.ds(c * N, N), :]
        re, im = y[:, :B], y[:, B:]
        hi, lo = halves(jnp.concatenate([re * cos - im * sin, im * cos + re * sin], axis=0))
        conv[pl.ds(c, N, C), :] = dot(last, jnp.concatenate([hi, lo, hi], axis=0))

    def blocks(ref):
        return ref[...].reshape(N, C, B)

    gated = blocks(q_feat) * (blocks(conv) + gain[None] * blocks(prod))
    o_send[...] = gated.astype(BF16).reshape(W, B)
    lax.fori_loop(0, N - 1, send_out, 0)
    o_recv[mine, :] = o_send[mine, :]

    most = pl.ds(0, (N - 1) * C)
    arrived(o_recv.at[most], recv_sems.at[4])
    for j in range(W // B):
        out_ref[:, j * B : (j + 1) * B] = o_recv[j * B : (j + 1) * B, :].T
    arrived(note_recv.at[pl.ds(0, N - 1)], send_sems.at[0])
    arrived(kv_send.at[pl.ds(0, N - 1)], send_sems.at[1])
    arrived(f_send.at[most], send_sems.at[2])
    arrived(q_send.at[pl.ds(0, N - 1)], send_sems.at[3])
    arrived(o_send.at[most], send_sems.at[4])


def body(loader_rows, row_pos, short_w, long_filter, skip_gain):
    first, twiddle, fwd, inv, last = (jnp.asarray(t) for t in tables())
    operands = [
        row_pos.reshape(1, B), loader_rows, long_filter, short_w, skip_gain.reshape(1, W),
        first, twiddle, last, fwd, inv,
    ]
    return pl.pallas_call(
        kernel,
        out_shape=pltpu.VMEM((B, W), BF16),
        in_specs=[pl.BlockSpec(memory_space=pltpu.HBM)] * ARGS,
        out_specs=pl.BlockSpec(memory_space=pltpu.VMEM),
        scratch_shapes=[
            *(pltpu.VMEM(x.shape, x.dtype) for x in operands),
            pltpu.VMEM((N, 2 * C, B), BF16),
            pltpu.VMEM((N, C, B), BF16),
            pltpu.VMEM((W, B), jnp.int16),
            pltpu.VMEM((W // B, 1, B), F32),
            pltpu.VMEM((N, 2 * C, B), BF16),
            pltpu.VMEM((N, C, B), BF16),
            pltpu.VMEM((W, B), jnp.int16),
            pltpu.VMEM((N, 1, B), F32),
            pltpu.VMEM((N, N * CAP, B), BF16),
            pltpu.VMEM((N, N * CAP, B), BF16),
            pltpu.VMEM((N, N * CAP, 2 * C), BF16),
            pltpu.VMEM((N, N * CAP, C), BF16),
            pltpu.VMEM((W, B), F32),
            pltpu.VMEM((W, B), F32),
            pltpu.VMEM((W, B), F32),
            pltpu.VMEM((W, 2 * B), F32),
            pltpu.VMEM((W, 2 * B), F32),
            pltpu.VMEM((W, B), F32),
            pltpu.VMEM((W, B), BF16),
            pltpu.VMEM((W, B), BF16),
            pltpu.SemaphoreType.DMA((5,)),
            pltpu.SemaphoreType.DMA((5,)),
            pltpu.SemaphoreType.DMA((N,)),
            pltpu.SemaphoreType.DMA((N,)),
            pltpu.SemaphoreType.DMA((ARGS,)),
        ],
        compiler_params=pltpu.CompilerParams(
            collective_id=0, has_side_effects=True, vmem_limit_bytes=54 << 20
        ),
    )(*operands)


def solution(mesh):
    return jax.shard_map(
        body,
        mesh=mesh,
        in_specs=(P("ctx", "chan"), P("ctx"), P(None, "chan"), P("ctx", "chan"), P("chan")),
        out_specs=P("ctx", "chan"),
        check_vma=False,
    )
```

```python
import functools
import math

import jax
import jax.numpy as jnp
import ml_dtypes
import numpy as np
from jax import lax
from jax.experimental import pallas as pl
from jax.experimental.pallas import tpu as pltpu
from jax.sharding import PartitionSpec as P

N = 32
B = 128
C = 16
W = 512
ARGS = 10
LEVEL = 32768.0
STEPS = 32767.0
CAP = 8
F32, BF16 = jnp.float32, jnp.bfloat16
NT = (((1,), (1,)), ((), ()))
TN = (((0,), (0,)), ((), ()))
NN = (((1,), (0,)), ((), ()))


def dot(a, b, dims=NN):
    return lax.dot_general(a, b, dims, preferred_element_type=F32)


def unit_of(level):
    return jnp.exp2((level - 512.0) * 0.25)


def halves(x):
    hi = x.astype(BF16)
    return hi, (x - hi.astype(F32)).astype(BF16)


def np_halves(x):
    hi = x.astype(ml_dtypes.bfloat16)
    return hi, (x - hi.astype(np.float64)).astype(ml_dtypes.bfloat16)


@functools.cache
def tables():
    quarter = np.arange(N) + 0.25
    block = 2 * math.pi * np.outer(quarter, np.arange(N)) / N
    turn = 2 * math.pi * np.outer(quarter, np.arange(B)) / (N * B)
    lane = 2 * math.pi * (np.outer(np.arange(B), np.arange(B)) % B) / B
    hi, lo = np_halves(np.concatenate([np.cos(block), -np.sin(block)]))
    first = np.concatenate([hi, hi, lo], axis=1)
    hi, lo = np_halves(np.concatenate([np.cos(block.T), -np.sin(block.T)], axis=1) / (N * B))
    last = np.concatenate([hi, hi, lo], axis=1)
    twiddle = np.stack([np.cos(turn), np.sin(turn)]).astype(np.float32)
    c, s = np.cos(lane), np.sin(lane)
    hi, lo = np_halves(np.block([[c, -s], [s, c]]))
    fwd = np.concatenate([hi, hi, lo])
    hi, lo = np_halves(np.block([[c, s], [-s, c]]))
    inv = np.concatenate([hi, hi, lo])
    return first, twiddle, fwd, inv, last


def iota(shape, dim):
    return lax.broadcasted_iota(jnp.int32, shape, dim)


def wide(z, g_ref):
    hi, lo = halves(z)
    return dot(jnp.concatenate([hi, lo, hi], axis=1), g_ref[...])


def partner(me, step):
    a = step // 8
    return me ^ (jnp.where(a < 2, 2 + a, 3 - a) * 8 + 7 - step % 8)


def forward(src, gain, first_ref, tw_ref, fwd_ref, dst):
    cos, sin = tw_ref[0], tw_ref[1]
    first = first_ref[...]
    for start in range(0, C, 2):
        group = range(start, start + 2)
        parts = [src[pl.ds(c, N, C), :] for c in group]
        if gain is not None:
            parts = [x * gain[:, c : c + 1] for c, x in zip(group, parts)]
        hi, lo = halves(jnp.concatenate(parts, axis=1))
        y = dot(first, jnp.concatenate([hi, lo, hi], axis=0))
        for i, c in enumerate(group):
            re, im = y[:N, i * B : (i + 1) * B], y[N:, i * B : (i + 1) * B]
            dst[pl.ds(c * N, N), :] = jnp.concatenate(
                [re * cos + im * sin, im * cos - re * sin], axis=1
            )
    dst[...] = wide(dst[...], fwd_ref)


def kernel(
    *refs,
):
    given, out_ref, here = refs[:ARGS], refs[ARGS], refs[ARGS + 1 : 2 * ARGS + 1]
    scratch, load_sems = refs[2 * ARGS + 1 : -1], refs[-1]
    loads = [
        pltpu.make_async_copy(given[i], here[i], load_sems.at[i]) for i in range(ARGS)
    ]
    work(loads, *here, out_ref, *scratch)


def work(
    loads,
    pos_ref, rows_ref, filt_ref, w_ref, gain_ref, first_ref, tw_ref, last_ref, fwd_ref, inv_ref,
    out_ref,
    kv_send, q_send, f_send, note_send, kv_recv, q_recv, f_recv, note_recv,
    onehot, place, kv_cand, q_cand, q_feat, prod, filt, spec_p, spec_f, conv, o_send, o_recv,
    send_sems, recv_sems, kv_sems, q_sems,
):
    me = lax.axis_index("ctx")
    barrier = pltpu.get_barrier_semaphore()

    def greet(step, _):
        pl.semaphore_signal(
            barrier,
            inc=1,
            device_id={"ctx": partner(me, step)},
            device_id_type=pl.DeviceIdType.MESH,
        )
        return 0

    lax.fori_loop(0, N - 1, greet, 0)
    for load in loads:
        load.start()

    loads[0].wait()
    pos = pos_ref[...]
    owner = pos // B
    across = jnp.broadcast_to(owner.astype(F32), (B, B))
    down = across.T
    earlier = (across == down) & (iota((B, B), 0) < iota((B, B), 1))
    rank = jnp.sum(jnp.where(earlier, 1.0, 0.0), axis=0, keepdims=True).astype(jnp.int32)
    code = ((owner * CAP + rank) * B + (pos - owner * B)).astype(F32)

    per = B // C

    def turned(part, j):
        return rows_ref[:, part * W + j * B : part * W + (j + 1) * B].T.reshape(per, C, B)

    loads[1].wait()
    for j in range(W // B):
        kv_send[j * per : (j + 1) * per, :C, :] = turned(1, j)
        kv_send[j * per : (j + 1) * per, C:, :] = turned(2, j)

    loads[2].wait()
    largest = jnp.maximum(jnp.max(jnp.abs(filt_ref[...]), axis=0, keepdims=True), 1e-33)
    level = jnp.clip(jnp.ceil(4.0 * jnp.log2(largest * (1.0 / STEPS))) + 512.0, 1.0, 510.0)
    level = jnp.where(unit_of(level) * STEPS < largest, level + 1.0, level)
    for j in range(W // B):
        note_send[j] = level[:, j * B : (j + 1) * B] * LEVEL + code
    mine = pl.ds(pl.multiple_of(me * C, C), C)
    note_recv[me] = note_send[me // per]

    pl.semaphore_wait(barrier, N - 1)

    def copy(src, dst, send_sem, recv_sem, to):
        return pltpu.make_async_remote_copy(
            src_ref=src,
            dst_ref=dst,
            send_sem=send_sem,
            recv_sem=recv_sem,
            device_id={"ctx": to},
            device_id_type=pl.DeviceIdType.MESH,
        )

    def send_note(step, _):
        to = partner(me, step)
        copy(note_send.at[to // per], note_recv.at[me], send_sems.at[0], recv_sems.at[0], to).start()
        return 0

    def send_kv(step, _):
        to = partner(me, step)
        copy(kv_send.at[to], kv_recv.at[step], send_sems.at[1], kv_sems.at[step], to).start()
        return 0

    def send_q(step, _):
        to = partner(me, step)
        copy(q_send.at[to], q_recv.at[step], send_sems.at[3], q_sems.at[step], to).start()
        return 0

    def channels_of(to):
        return pl.ds(pl.multiple_of(to * C, C), C)

    def send_filter(step, _):
        to = partner(me, step)
        copy(f_send.at[channels_of(to), :], f_recv.at[mine, :], send_sems.at[2], recv_sems.at[2], to).start()
        return 0

    def send_out(step, _):
        to = partner(me, step)
        copy(o_send.at[channels_of(to), :], o_recv.at[mine, :], send_sems.at[4], recv_sems.at[4], to).start()
        return 0

    lax.fori_loop(0, N - 1, send_note, 0)
    lax.fori_loop(0, N - 1, send_kv, 0)
    pltpu.make_async_copy(kv_send.at[me], kv_recv.at[N - 1], kv_sems.at[N - 1]).start()

    for j in range(W // B):
        q_send[j * per : (j + 1) * per] = turned(0, j)
    lax.fori_loop(0, N - 1, send_q, 0)
    pltpu.make_async_copy(q_send.at[me], q_recv.at[N - 1], q_sems.at[N - 1]).start()

    per_unit = 1.0 / unit_of(level)
    for j in range(W // B):
        part = slice(j * B, (j + 1) * B)
        steps = jnp.round(filt_ref[:, part] * per_unit[:, part]).T
        f_send[part, :] = steps.astype(jnp.int32).astype(jnp.int16)
    lax.fori_loop(0, N - 1, send_filter, 0)
    f_recv[mine, :] = f_send[mine, :]

    def arrived(part, sem):
        pltpu.make_async_copy(part, part, sem).wait()

    for load in loads[3:]:
        load.wait()

    pick = iota((C, W), 1) == me * C + iota((C, W), 0)

    def column(row):
        return jnp.sum(jnp.where(pick, row, 0.0), axis=1, keepdims=True)

    q_taps, k_taps, v_taps = (
        [column(w_ref[i : i + 1, p * W : (p + 1) * W]) for i in range(3)] for p in range(3)
    )
    kv_taps = [jnp.concatenate([k, v], axis=0) for k, v in zip(k_taps, v_taps)]
    gain = column(gain_ref[...])

    arrived(note_recv.at[pl.ds(0, N - 1)], recv_sems.at[0])

    def pair(h):
        return pl.ds(pl.multiple_of(h * 2 * CAP, 2 * CAP), 2 * CAP)

    def index(h, _):
        tiles = []
        for k in (2 * h, 2 * h + 1):
            note = note_recv[partner(me, k)]
            code = (note - jnp.floor(note * (1.0 / LEVEL)) * LEVEL).astype(jnp.int32)
            slot = code // B
            within = (code - slot * B + 1).astype(F32)
            hot = (iota((N * CAP, B), 0) == slot).astype(F32).astype(BF16)
            onehot[k] = hot
            at = dot(hot, jnp.broadcast_to(within, (B, B)).astype(BF16), NT)
            tile = (at == (iota((N * CAP, B), 1) + 1).astype(F32)).astype(F32)
            tiles.append(tile.reshape(N, CAP, B))
        place[:, pair(h), :] = jnp.concatenate(tiles, axis=1).astype(BF16)
        return 0

    lax.fori_loop(0, N // 2, index, 0, unroll=4)

    def spread(recv, sems, cand):
        def group(g, _):
            for i in range(8):
                k = g * 8 + i
                arrived(recv.at[k], sems.at[k])
            for i in range(4):
                h = g * 4 + i
                tiles = [
                    dot(onehot[k], recv[k], NT).reshape(N, CAP, recv.shape[1])
                    for k in (2 * h, 2 * h + 1)
                ]
                cand[:, pair(h), :] = jnp.concatenate(tiles, axis=1).astype(BF16)
            return 0

        lax.fori_loop(0, N // 8, group, 0)

    def filtered(taps, before, seq):
        lane = iota(seq.shape, 1)
        feat = taps[0] * seq
        for i in (1, 2):
            moved = jnp.where(lane < i, pltpu.roll(before, i, 1), pltpu.roll(seq, i, 1))
            feat = feat + taps[i] * moved
        return feat

    spread(kv_recv, kv_sems, kv_cand)

    def block(o, before):
        seq = dot(kv_cand[o], place[o], TN)
        feat = filtered(kv_taps, before, seq)
        prod[pl.ds(pl.multiple_of(o * C, C), C), :] = feat[:C] * feat[C:]
        return seq

    lax.fori_loop(0, N, block, jnp.zeros((2 * C, B), F32), unroll=8)

    forward(prod, None, first_ref, tw_ref, fwd_ref, spec_p)

    spread(q_recv, q_sems, q_cand)

    def q_block(o, before):
        seq = dot(q_cand[o], place[o], TN)
        q_feat[pl.ds(pl.multiple_of(o * C, C), C), :] = filtered(q_taps, before, seq)
        return seq

    lax.fori_loop(0, N, q_block, jnp.zeros((C, B), F32), unroll=8)

    arrived(f_recv.at[pl.ds(0, (N - 1) * C)], recv_sems.at[2])
    filt[...] = f_recv[...].astype(jnp.int32).astype(F32)
    units = unit_of(jnp.floor(note_recv[:, 0, :] * (1.0 / LEVEL)))
    units = pltpu.roll(units, lax.rem(B - lax.rem(me, per) * C, B), 1)
    forward(filt, units, first_ref, tw_ref, fwd_ref, spec_f)

    a_re, a_im = spec_p[:, :B], spec_p[:, B:]
    b_re, b_im = spec_f[:, :B], spec_f[:, B:]
    z = jnp.concatenate([a_re * b_re - a_im * b_im, a_re * b_im + a_im * b_re], axis=1)
    spec_p[...] = wide(z, inv_ref)
    cos, sin = tw_ref[0], tw_ref[1]
    last = last_ref[...]
    for start in range(0, C, 2):
        group = range(start, start + 2)
        parts = []
        for c in group:
            y = spec_p[pl.ds(c * N, N), :]
            re, im = y[:, :B], y[:, B:]
            parts.append(jnp.concatenate([re * cos - im * sin, im * cos + re * sin], axis=0))
        hi, lo = halves(jnp.concatenate(parts, axis=1))
        y = dot(last, jnp.concatenate([hi, lo, hi], axis=0))
        for i, c in enumerate(group):
            conv[pl.ds(c, N, C), :] = y[:, i * B : (i + 1) * B]

    def blocks(ref):
        return ref[...].reshape(N, C, B)

    gated = blocks(q_feat) * (blocks(conv) + gain[None] * blocks(prod))
    o_send[...] = gated.astype(BF16).reshape(W, B)
    lax.fori_loop(0, N - 1, send_out, 0)
    o_recv[mine, :] = o_send[mine, :]

    most = pl.ds(0, (N - 1) * C)
    arrived(o_recv.at[most], recv_sems.at[4])
    for j in range(W // B):
        out_ref[:, j * B : (j + 1) * B] = o_recv[j * B : (j + 1) * B, :].T
    arrived(note_recv.at[pl.ds(0, N - 1)], send_sems.at[0])
    arrived(kv_send.at[pl.ds(0, N - 1)], send_sems.at[1])
    arrived(f_send.at[most], send_sems.at[2])
    arrived(q_send.at[pl.ds(0, N - 1)], send_sems.at[3])
    arrived(o_send.at[most], send_sems.at[4])


def body(loader_rows, row_pos, short_w, long_filter, skip_gain):
    first, twiddle, fwd, inv, last = (jnp.asarray(t) for t in tables())
    operands = [
        row_pos.reshape(1, B), loader_rows, long_filter, short_w, skip_gain.reshape(1, W),
        first, twiddle, last, fwd, inv,
    ]
    return pl.pallas_call(
        kernel,
        out_shape=pltpu.VMEM((B, W), BF16),
        in_specs=[pl.BlockSpec(memory_space=pltpu.HBM)] * ARGS,
        out_specs=pl.BlockSpec(memory_space=pltpu.VMEM),
        scratch_shapes=[
            *(pltpu.VMEM(x.shape, x.dtype) for x in operands),
            pltpu.VMEM((N, 2 * C, B), BF16),
            pltpu.VMEM((N, C, B), BF16),
            pltpu.VMEM((W, B), jnp.int16),
            pltpu.VMEM((W // B, 1, B), F32),
            pltpu.VMEM((N, 2 * C, B), BF16),
            pltpu.VMEM((N, C, B), BF16),
            pltpu.VMEM((W, B), jnp.int16),
            pltpu.VMEM((N, 1, B), F32),
            pltpu.VMEM((N, N * CAP, B), BF16),
            pltpu.VMEM((N, N * CAP, B), BF16),
            pltpu.VMEM((N, N * CAP, 2 * C), BF16),
            pltpu.VMEM((N, N * CAP, C), BF16),
            pltpu.VMEM((W, B), F32),
            pltpu.VMEM((W, B), F32),
            pltpu.VMEM((W, B), F32),
            pltpu.VMEM((W, 2 * B), F32),
            pltpu.VMEM((W, 2 * B), F32),
            pltpu.VMEM((W, B), F32),
            pltpu.VMEM((W, B), BF16),
            pltpu.VMEM((W, B), BF16),
            pltpu.SemaphoreType.DMA((5,)),
            pltpu.SemaphoreType.DMA((5,)),
            pltpu.SemaphoreType.DMA((N,)),
            pltpu.SemaphoreType.DMA((N,)),
            pltpu.SemaphoreType.DMA((ARGS,)),
        ],
        compiler_params=pltpu.CompilerParams(
            collective_id=0, has_side_effects=True, vmem_limit_bytes=54 << 20
        ),
    )(*operands)


def solution(mesh):
    return jax.shard_map(
        body,
        mesh=mesh,
        in_specs=(P("ctx", "chan"), P("ctx"), P(None, "chan"), P("ctx", "chan"), P("chan")),
        out_specs=P("ctx", "chan"),
        check_vma=False,
    )
```

```python
import functools
import math

import jax
import jax.numpy as jnp
import ml_dtypes
import numpy as np
from jax import lax
from jax.experimental import pallas as pl
from jax.experimental.pallas import tpu as pltpu
from jax.sharding import PartitionSpec as P

N = 32
B = 128
C = 16
W = 512
ARGS = 10
LEVEL = 32768.0
STEPS = 32767.0
CAP = 8
F32, BF16 = jnp.float32, jnp.bfloat16
NT = (((1,), (1,)), ((), ()))
TN = (((0,), (0,)), ((), ()))
NN = (((1,), (0,)), ((), ()))


def dot(a, b, dims=NN):
    return lax.dot_general(a, b, dims, preferred_element_type=F32)


def unit_of(level):
    return jnp.exp2((level - 512.0) * 0.25)


def halves(x):
    hi = x.astype(BF16)
    return hi, (x - hi.astype(F32)).astype(BF16)


def np_halves(x):
    hi = x.astype(ml_dtypes.bfloat16)
    return hi, (x - hi.astype(np.float64)).astype(ml_dtypes.bfloat16)


@functools.cache
def tables():
    quarter = np.arange(N) + 0.25
    block = 2 * math.pi * np.outer(quarter, np.arange(N)) / N
    turn = 2 * math.pi * np.outer(quarter, np.arange(B)) / (N * B)
    lane = 2 * math.pi * (np.outer(np.arange(B), np.arange(B)) % B) / B
    hi, lo = np_halves(np.concatenate([np.cos(block), -np.sin(block)]))
    first = np.concatenate([hi, hi, lo], axis=1)
    hi, lo = np_halves(np.concatenate([np.cos(block.T), -np.sin(block.T)], axis=1) / (N * B))
    last = np.concatenate([hi, hi, lo], axis=1)
    twiddle = np.stack([np.cos(turn), np.sin(turn)]).astype(np.float32)
    c, s = np.cos(lane), np.sin(lane)
    hi, lo = np_halves(np.block([[c, -s], [s, c]]))
    fwd = np.concatenate([hi, hi, lo])
    hi, lo = np_halves(np.block([[c, s], [-s, c]]))
    inv = np.concatenate([hi, hi, lo])
    return first, twiddle, fwd, inv, last


def iota(shape, dim):
    return lax.broadcasted_iota(jnp.int32, shape, dim)


def wide(z, g_ref):
    hi, lo = halves(z)
    return dot(jnp.concatenate([hi, lo, hi], axis=1), g_ref[...])


def partner(me, step):
    a = step // 8
    return me ^ (jnp.where(a < 2, 2 + a, 3 - a) * 8 + 7 - step % 8)


def forward(src, gain, first_ref, tw_ref, fwd_ref, dst):
    cos, sin = tw_ref[0], tw_ref[1]
    first = first_ref[...]
    for start in range(0, C, 2):
        group = range(start, start + 2)
        parts = [src[pl.ds(c, N, C), :] for c in group]
        if gain is not None:
            parts = [x * gain[:, c : c + 1] for c, x in zip(group, parts)]
        hi, lo = halves(jnp.concatenate(parts, axis=1))
        y = dot(first, jnp.concatenate([hi, lo, hi], axis=0))
        for i, c in enumerate(group):
            re, im = y[:N, i * B : (i + 1) * B], y[N:, i * B : (i + 1) * B]
            dst[pl.ds(c * N, N), :] = jnp.concatenate(
                [re * cos + im * sin, im * cos - re * sin], axis=1
            )
    dst[...] = wide(dst[...], fwd_ref)


def kernel(
    *refs,
):
    given, out_ref, here = refs[:ARGS], refs[ARGS], refs[ARGS + 1 : 2 * ARGS + 1]
    scratch, load_sems = refs[2 * ARGS + 1 : -1], refs[-1]
    loads = [
        pltpu.make_async_copy(given[i], here[i], load_sems.at[i]) for i in range(ARGS)
    ]
    work(loads, *here, out_ref, *scratch)


def work(
    loads,
    pos_ref, rows_ref, filt_ref, w_ref, gain_ref, first_ref, tw_ref, last_ref, fwd_ref, inv_ref,
    out_ref,
    kv_send, q_send, f_send, note_send, kv_recv, q_recv, f_recv, note_recv,
    onehot, place, kv_cand, q_cand, q_feat, prod, filt, spec_p, spec_f, conv, o_send, o_recv,
    send_sems, recv_sems, kv_sems, q_sems,
):
    me = lax.axis_index("ctx")
    barrier = pltpu.get_barrier_semaphore()

    def greet(step, _):
        pl.semaphore_signal(
            barrier,
            inc=1,
            device_id={"ctx": partner(me, step)},
            device_id_type=pl.DeviceIdType.MESH,
        )
        return 0

    lax.fori_loop(0, N - 1, greet, 0)
    for load in loads:
        load.start()

    loads[0].wait()
    pos = pos_ref[...]
    owner = pos // B
    across = jnp.broadcast_to(owner.astype(F32), (B, B))
    down = across.T
    earlier = (across == down) & (iota((B, B), 0) < iota((B, B), 1))
    rank = jnp.sum(jnp.where(earlier, 1.0, 0.0), axis=0, keepdims=True).astype(jnp.int32)
    code = ((owner * CAP + rank) * B + (pos - owner * B)).astype(F32)

    per = B // C

    def turned(part, j):
        return rows_ref[:, part * W + j * B : part * W + (j + 1) * B].T.reshape(per, C, B)

    loads[1].wait()
    for j in range(W // B):
        kv_send[j * per : (j + 1) * per, :C, :] = turned(1, j)
        kv_send[j * per : (j + 1) * per, C:, :] = turned(2, j)

    loads[2].wait()
    largest = jnp.maximum(jnp.max(jnp.abs(filt_ref[...]), axis=0, keepdims=True), 1e-33)
    level = jnp.clip(jnp.ceil(4.0 * jnp.log2(largest * (1.0 / STEPS))) + 512.0, 1.0, 510.0)
    level = jnp.where(unit_of(level) * STEPS < largest, level + 1.0, level)
    for j in range(W // B):
        note_send[j] = level[:, j * B : (j + 1) * B] * LEVEL + code
    mine = pl.ds(pl.multiple_of(me * C, C), C)
    note_recv[me] = note_send[me // per]

    pl.semaphore_wait(barrier, N - 1)

    def copy(src, dst, send_sem, recv_sem, to):
        return pltpu.make_async_remote_copy(
            src_ref=src,
            dst_ref=dst,
            send_sem=send_sem,
            recv_sem=recv_sem,
            device_id={"ctx": to},
            device_id_type=pl.DeviceIdType.MESH,
        )

    def send_note(step, _):
        to = partner(me, step)
        copy(note_send.at[to // per], note_recv.at[me], send_sems.at[0], recv_sems.at[0], to).start()
        return 0

    def send_kv(step, _):
        to = partner(me, step)
        copy(kv_send.at[to], kv_recv.at[step], send_sems.at[1], kv_sems.at[step], to).start()
        return 0

    def send_q(step, _):
        to = partner(me, step)
        copy(q_send.at[to], q_recv.at[step], send_sems.at[3], q_sems.at[step], to).start()
        return 0

    def channels_of(to):
        return pl.ds(pl.multiple_of(to * C, C), C)

    def send_filter(step, _):
        to = partner(me, step)
        copy(f_send.at[channels_of(to), :], f_recv.at[mine, :], send_sems.at[2], recv_sems.at[2], to).start()
        return 0

    def send_out(step, _):
        to = partner(me, step)
        copy(o_send.at[channels_of(to), :], o_recv.at[mine, :], send_sems.at[4], recv_sems.at[4], to).start()
        return 0

    lax.fori_loop(0, N - 1, send_note, 0)
    lax.fori_loop(0, N - 1, send_kv, 0)
    pltpu.make_async_copy(kv_send.at[me], kv_recv.at[N - 1], kv_sems.at[N - 1]).start()

    for j in range(W // B):
        q_send[j * per : (j + 1) * per] = turned(0, j)
    lax.fori_loop(0, N - 1, send_q, 0)
    pltpu.make_async_copy(q_send.at[me], q_recv.at[N - 1], q_sems.at[N - 1]).start()

    per_unit = 1.0 / unit_of(level)
    for j in range(W // B):
        part = slice(j * B, (j + 1) * B)
        steps = jnp.round(filt_ref[:, part] * per_unit[:, part]).T
        f_send[part, :] = steps.astype(jnp.int32).astype(jnp.int16)
    lax.fori_loop(0, N - 1, send_filter, 0)
    f_recv[mine, :] = f_send[mine, :]

    def arrived(part, sem):
        pltpu.make_async_copy(part, part, sem).wait()

    for load in loads[3:]:
        load.wait()

    pick = iota((C, W), 1) == me * C + iota((C, W), 0)

    def column(row):
        return jnp.sum(jnp.where(pick, row, 0.0), axis=1, keepdims=True)

    q_taps, k_taps, v_taps = (
        [column(w_ref[i : i + 1, p * W : (p + 1) * W]) for i in range(3)] for p in range(3)
    )
    kv_taps = [jnp.concatenate([k, v], axis=0) for k, v in zip(k_taps, v_taps)]
    gain = column(gain_ref[...])

    arrived(note_recv.at[pl.ds(0, N - 1)], recv_sems.at[0])

    def pair(h):
        return pl.ds(pl.multiple_of(h * 2 * CAP, 2 * CAP), 2 * CAP)

    def index(h, _):
        tiles = []
        for k in (2 * h, 2 * h + 1):
            note = note_recv[partner(me, k)]
            code = (note - jnp.floor(note * (1.0 / LEVEL)) * LEVEL).astype(jnp.int32)
            slot = code // B
            within = (code - slot * B + 1).astype(F32)
            hot = (iota((N * CAP, B), 0) == slot).astype(F32).astype(BF16)
            onehot[k] = hot
            at = dot(hot, jnp.broadcast_to(within, (B, B)).astype(BF16), NT)
            tile = (at == (iota((N * CAP, B), 1) + 1).astype(F32)).astype(F32)
            tiles.append(tile.reshape(N, CAP, B))
        place[:, pair(h), :] = jnp.concatenate(tiles, axis=1).astype(BF16)
        return 0

    lax.fori_loop(0, N // 2, index, 0, unroll=4)

    def spread(recv, sems, cand):
        def group(g, _):
            for i in range(8):
                k = g * 8 + i
                arrived(recv.at[k], sems.at[k])
            for i in range(4):
                h = g * 4 + i
                tiles = [
                    dot(onehot[k], recv[k], NT).reshape(N, CAP, recv.shape[1])
                    for k in (2 * h, 2 * h + 1)
                ]
                cand[:, pair(h), :] = jnp.concatenate(tiles, axis=1).astype(BF16)
            return 0

        lax.fori_loop(0, N // 8, group, 0)

    def filtered(taps, before, seq):
        lane = iota(seq.shape, 1)
        feat = taps[0] * seq
        for i in (1, 2):
            moved = jnp.where(lane < i, pltpu.roll(before, i, 1), pltpu.roll(seq, i, 1))
            feat = feat + taps[i] * moved
        return feat

    spread(kv_recv, kv_sems, kv_cand)

    def block(o, before):
        seq = dot(kv_cand[o], place[o], TN)
        feat = filtered(kv_taps, before, seq)
        prod[pl.ds(pl.multiple_of(o * C, C), C), :] = feat[:C] * feat[C:]
        return seq

    lax.fori_loop(0, N, block, jnp.zeros((2 * C, B), F32), unroll=8)

    forward(prod, None, first_ref, tw_ref, fwd_ref, spec_p)

    spread(q_recv, q_sems, q_cand)

    def q_block(o, before):
        seq = dot(q_cand[o], place[o], TN)
        q_feat[pl.ds(pl.multiple_of(o * C, C), C), :] = filtered(q_taps, before, seq)
        return seq

    lax.fori_loop(0, N, q_block, jnp.zeros((C, B), F32), unroll=8)

    arrived(f_recv.at[pl.ds(0, (N - 1) * C)], recv_sems.at[2])
    filt[...] = f_recv[...].astype(jnp.int32).astype(F32)
    units = unit_of(jnp.floor(note_recv[:, 0, :] * (1.0 / LEVEL)))
    units = pltpu.roll(units, lax.rem(B - lax.rem(me, per) * C, B), 1)
    forward(filt, units, first_ref, tw_ref, fwd_ref, spec_f)

    a_re, a_im = spec_p[:, :B], spec_p[:, B:]
    b_re, b_im = spec_f[:, :B], spec_f[:, B:]
    z = jnp.concatenate([a_re * b_re - a_im * b_im, a_re * b_im + a_im * b_re], axis=1)
    spec_p[...] = wide(z, inv_ref)
    cos, sin = tw_ref[0], tw_ref[1]
    last = last_ref[...]
    for start in range(0, C, 2):
        group = range(start, start + 2)
        parts = []
        for c in group:
            y = spec_p[pl.ds(c * N, N), :]
            re, im = y[:, :B], y[:, B:]
            parts.append(jnp.concatenate([re * cos - im * sin, im * cos + re * sin], axis=0))
        hi, lo = halves(jnp.concatenate(parts, axis=1))
        y = dot(last, jnp.concatenate([hi, lo, hi], axis=0))
        for i, c in enumerate(group):
            conv[pl.ds(c, N, C), :] = y[:, i * B : (i + 1) * B]

    for start in range(0, N, 8):
        first_owner = partner(me, start) // 8 * 8
        plane = pl.ds(pl.multiple_of(first_owner * C, 8 * C), 8 * C)

        def blocks(ref):
            return ref[plane, :].reshape(8, C, B)

        gated = blocks(q_feat) * (blocks(conv) + gain[None] * blocks(prod))
        o_send[plane, :] = gated.astype(BF16).reshape(8 * C, B)
        lax.fori_loop(start, min(start + 8, N - 1), send_out, 0)
    o_recv[mine, :] = o_send[mine, :]

    most = pl.ds(0, (N - 1) * C)
    arrived(o_recv.at[most], recv_sems.at[4])
    out_ref[...] = o_recv[...]
    arrived(note_recv.at[pl.ds(0, N - 1)], send_sems.at[0])
    arrived(kv_send.at[pl.ds(0, N - 1)], send_sems.at[1])
    arrived(f_send.at[most], send_sems.at[2])
    arrived(q_send.at[pl.ds(0, N - 1)], send_sems.at[3])
    arrived(o_send.at[most], send_sems.at[4])


def body(loader_rows, row_pos, short_w, long_filter, skip_gain):
    first, twiddle, fwd, inv, last = (jnp.asarray(t) for t in tables())
    operands = [
        row_pos.reshape(1, B), loader_rows, long_filter, short_w, skip_gain.reshape(1, W),
        first, twiddle, last, fwd, inv,
    ]
    turned = pl.pallas_call(
        kernel,
        out_shape=pltpu.VMEM((W, B), BF16),
        in_specs=[pl.BlockSpec(memory_space=pltpu.HBM)] * ARGS,
        out_specs=pl.BlockSpec(memory_space=pltpu.VMEM),
        scratch_shapes=[
            *(pltpu.VMEM(x.shape, x.dtype) for x in operands),
            pltpu.VMEM((N, 2 * C, B), BF16),
            pltpu.VMEM((N, C, B), BF16),
            pltpu.VMEM((W, B), jnp.int16),
            pltpu.VMEM((W // B, 1, B), F32),
            pltpu.VMEM((N, 2 * C, B), BF16),
            pltpu.VMEM((N, C, B), BF16),
            pltpu.VMEM((W, B), jnp.int16),
            pltpu.VMEM((N, 1, B), F32),
            pltpu.VMEM((N, N * CAP, B), BF16),
            pltpu.VMEM((N, N * CAP, B), BF16),
            pltpu.VMEM((N, N * CAP, 2 * C), BF16),
            pltpu.VMEM((N, N * CAP, C), BF16),
            pltpu.VMEM((W, B), F32),
            pltpu.VMEM((W, B), F32),
            pltpu.VMEM((W, B), F32),
            pltpu.VMEM((W, 2 * B), F32),
            pltpu.VMEM((W, 2 * B), F32),
            pltpu.VMEM((W, B), F32),
            pltpu.VMEM((W, B), BF16),
            pltpu.VMEM((W, B), BF16),
            pltpu.SemaphoreType.DMA((5,)),
            pltpu.SemaphoreType.DMA((5,)),
            pltpu.SemaphoreType.DMA((N,)),
            pltpu.SemaphoreType.DMA((N,)),
            pltpu.SemaphoreType.DMA((ARGS,)),
        ],
        compiler_params=pltpu.CompilerParams(
            collective_id=0, has_side_effects=True, vmem_limit_bytes=54 << 20
        ),
    )(*operands)
    return turned.T


def solution(mesh):
    return jax.shard_map(
        body,
        mesh=mesh,
        in_specs=(P("ctx", "chan"), P("ctx"), P(None, "chan"), P("ctx", "chan"), P("chan")),
        out_specs=P("ctx", "chan"),
        check_vma=False,
    )
```

```python
import functools
import math

import jax
import jax.numpy as jnp
import ml_dtypes
import numpy as np
from jax import lax
from jax.experimental import pallas as pl
from jax.experimental.pallas import tpu as pltpu
from jax.sharding import PartitionSpec as P

N = 32
B = 128
C = 16
W = 512
ARGS = 10
LEVEL = 32768.0
STEPS = 32767.0
CAP = 8
F32, BF16 = jnp.float32, jnp.bfloat16
NT = (((1,), (1,)), ((), ()))
TN = (((0,), (0,)), ((), ()))
NN = (((1,), (0,)), ((), ()))


def dot(a, b, dims=NN):
    return lax.dot_general(a, b, dims, preferred_element_type=F32)


def unit_of(level):
    return jnp.exp2((level - 512.0) * 0.25)


def halves(x):
    hi = x.astype(BF16)
    return hi, (x - hi.astype(F32)).astype(BF16)


def np_halves(x):
    hi = x.astype(ml_dtypes.bfloat16)
    return hi, (x - hi.astype(np.float64)).astype(ml_dtypes.bfloat16)


@functools.cache
def tables():
    quarter = np.arange(N) + 0.25
    block = 2 * math.pi * np.outer(quarter, np.arange(N)) / N
    turn = 2 * math.pi * np.outer(quarter, np.arange(B)) / (N * B)
    lane = 2 * math.pi * (np.outer(np.arange(B), np.arange(B)) % B) / B
    hi, lo = np_halves(np.concatenate([np.cos(block), -np.sin(block)]))
    first = np.concatenate([hi, hi, lo], axis=1)
    hi, lo = np_halves(np.concatenate([np.cos(block.T), -np.sin(block.T)], axis=1) / (N * B))
    last = np.concatenate([hi, hi, lo], axis=1)
    twiddle = np.stack([np.cos(turn), np.sin(turn)]).astype(np.float32)
    c, s = np.cos(lane), np.sin(lane)
    hi, lo = np_halves(np.block([[c, -s], [s, c]]))
    fwd = np.concatenate([hi, hi, lo])
    hi, lo = np_halves(np.block([[c, s], [-s, c]]))
    inv = np.concatenate([hi, hi, lo])
    return first, twiddle, fwd, inv, last


def iota(shape, dim):
    return lax.broadcasted_iota(jnp.int32, shape, dim)


def wide(z, g_ref):
    hi, lo = halves(z)
    return dot(jnp.concatenate([hi, lo, hi], axis=1), g_ref[...])


def partner(me, step):
    a = step // 8
    return me ^ (jnp.where(a < 2, 2 + a, 3 - a) * 8 + 7 - step % 8)


def forward(src, gain, first_ref, tw_ref, fwd_ref, dst):
    cos, sin = tw_ref[0], tw_ref[1]
    first = first_ref[...]
    for start in range(0, C, 2):
        group = range(start, start + 2)
        parts = [src[pl.ds(c, N, C), :] for c in group]
        if gain is not None:
            parts = [x * gain[:, c : c + 1] for c, x in zip(group, parts)]
        hi, lo = halves(jnp.concatenate(parts, axis=1))
        y = dot(first, jnp.concatenate([hi, lo, hi], axis=0))
        for i, c in enumerate(group):
            re, im = y[:N, i * B : (i + 1) * B], y[N:, i * B : (i + 1) * B]
            dst[pl.ds(c * N, N), :] = jnp.concatenate(
                [re * cos + im * sin, im * cos - re * sin], axis=1
            )
    dst[...] = wide(dst[...], fwd_ref)


def kernel(
    *refs,
):
    given, out_ref, here = refs[:ARGS], refs[ARGS], refs[ARGS + 1 : 2 * ARGS + 1]
    scratch, load_sems = refs[2 * ARGS + 1 : -1], refs[-1]
    loads = [
        pltpu.make_async_copy(given[i], here[i], load_sems.at[i]) for i in range(ARGS)
    ]
    work(loads, *here, out_ref, *scratch)


def work(
    loads,
    pos_ref, rows_ref, filt_ref, w_ref, gain_ref, first_ref, tw_ref, last_ref, fwd_ref, inv_ref,
    out_ref,
    kv_send, q_send, f_send, note_send, kv_recv, q_recv, f_recv, note_recv,
    onehot, place, kv_cand, q_cand, q_feat, prod, filt, spec_p, spec_f, conv, o_send,
    send_sems, recv_sems, kv_sems, q_sems,
):
    me = lax.axis_index("ctx")
    barrier = pltpu.get_barrier_semaphore()

    def greet(step, _):
        pl.semaphore_signal(
            barrier,
            inc=1,
            device_id={"ctx": partner(me, step)},
            device_id_type=pl.DeviceIdType.MESH,
        )
        return 0

    lax.fori_loop(0, N - 1, greet, 0)
    for load in loads:
        load.start()

    loads[0].wait()
    pos = pos_ref[...]
    owner = pos // B
    across = jnp.broadcast_to(owner.astype(F32), (B, B))
    down = across.T
    earlier = (across == down) & (iota((B, B), 0) < iota((B, B), 1))
    rank = jnp.sum(jnp.where(earlier, 1.0, 0.0), axis=0, keepdims=True).astype(jnp.int32)
    code = ((owner * CAP + rank) * B + (pos - owner * B)).astype(F32)

    per = B // C

    def turned(part, j):
        return rows_ref[:, part * W + j * B : part * W + (j + 1) * B].T.reshape(per, C, B)

    loads[1].wait()
    for j in range(W // B):
        kv_send[j * per : (j + 1) * per, :C, :] = turned(1, j)
        kv_send[j * per : (j + 1) * per, C:, :] = turned(2, j)

    loads[2].wait()
    largest = jnp.maximum(jnp.max(jnp.abs(filt_ref[...]), axis=0, keepdims=True), 1e-33)
    level = jnp.clip(jnp.ceil(4.0 * jnp.log2(largest * (1.0 / STEPS))) + 512.0, 1.0, 510.0)
    level = jnp.where(unit_of(level) * STEPS < largest, level + 1.0, level)
    for j in range(W // B):
        note_send[j] = level[:, j * B : (j + 1) * B] * LEVEL + code
    mine = pl.ds(pl.multiple_of(me * C, C), C)
    note_recv[me] = note_send[me // per]

    pl.semaphore_wait(barrier, N - 1)

    def copy(src, dst, send_sem, recv_sem, to):
        return pltpu.make_async_remote_copy(
            src_ref=src,
            dst_ref=dst,
            send_sem=send_sem,
            recv_sem=recv_sem,
            device_id={"ctx": to},
            device_id_type=pl.DeviceIdType.MESH,
        )

    def send_note(step, _):
        to = partner(me, step)
        copy(note_send.at[to // per], note_recv.at[me], send_sems.at[0], recv_sems.at[0], to).start()
        return 0

    def send_kv(step, _):
        to = partner(me, step)
        copy(kv_send.at[to], kv_recv.at[step], send_sems.at[1], kv_sems.at[step], to).start()
        return 0

    def send_q(step, _):
        to = partner(me, step)
        copy(q_send.at[to], q_recv.at[step], send_sems.at[3], q_sems.at[step], to).start()
        return 0

    def channels_of(to):
        return pl.ds(pl.multiple_of(to * C, C), C)

    def send_filter(step, _):
        to = partner(me, step)
        copy(f_send.at[channels_of(to), :], f_recv.at[mine, :], send_sems.at[2], recv_sems.at[2], to).start()
        return 0

    def send_out(step, _):
        to = partner(me, step)
        copy(o_send.at[channels_of(to), :], out_ref.at[mine, :], send_sems.at[4], recv_sems.at[4], to).start()
        return 0

    lax.fori_loop(0, N - 1, send_note, 0)
    lax.fori_loop(0, N - 1, send_kv, 0)
    pltpu.make_async_copy(kv_send.at[me], kv_recv.at[N - 1], kv_sems.at[N - 1]).start()

    for j in range(W // B):
        q_send[j * per : (j + 1) * per] = turned(0, j)
    lax.fori_loop(0, N - 1, send_q, 0)
    pltpu.make_async_copy(q_send.at[me], q_recv.at[N - 1], q_sems.at[N - 1]).start()

    per_unit = 1.0 / unit_of(level)
    for j in range(W // B):
        part = slice(j * B, (j + 1) * B)
        steps = jnp.round(filt_ref[:, part] * per_unit[:, part]).T
        f_send[part, :] = steps.astype(jnp.int32).astype(jnp.int16)
    lax.fori_loop(0, N - 1, send_filter, 0)
    f_recv[mine, :] = f_send[mine, :]

    def arrived(part, sem):
        pltpu.make_async_copy(part, part, sem).wait()

    for load in loads[3:]:
        load.wait()

    pick = iota((C, W), 1) == me * C + iota((C, W), 0)

    def column(row):
        return jnp.sum(jnp.where(pick, row, 0.0), axis=1, keepdims=True)

    q_taps, k_taps, v_taps = (
        [column(w_ref[i : i + 1, p * W : (p + 1) * W]) for i in range(3)] for p in range(3)
    )
    kv_taps = [jnp.concatenate([k, v], axis=0) for k, v in zip(k_taps, v_taps)]
    gain = column(gain_ref[...])

    arrived(note_recv.at[pl.ds(0, N - 1)], recv_sems.at[0])

    def pair(h):
        return pl.ds(pl.multiple_of(h * 2 * CAP, 2 * CAP), 2 * CAP)

    def index(h, _):
        tiles = []
        for k in (2 * h, 2 * h + 1):
            note = note_recv[partner(me, k)]
            code = (note - jnp.floor(note * (1.0 / LEVEL)) * LEVEL).astype(jnp.int32)
            slot = code // B
            within = (code - slot * B + 1).astype(F32)
            hot = (iota((N * CAP, B), 0) == slot).astype(F32).astype(BF16)
            onehot[k] = hot
            at = dot(hot, jnp.broadcast_to(within, (B, B)).astype(BF16), NT)
            tile = (at == (iota((N * CAP, B), 1) + 1).astype(F32)).astype(F32)
            tiles.append(tile.reshape(N, CAP, B))
        place[:, pair(h), :] = jnp.concatenate(tiles, axis=1).astype(BF16)
        return 0

    lax.fori_loop(0, N // 2, index, 0, unroll=4)

    def spread(recv, sems, cand):
        def group(g, _):
            for i in range(8):
                k = g * 8 + i
                arrived(recv.at[k], sems.at[k])
            for i in range(4):
                h = g * 4 + i
                tiles = [
                    dot(onehot[k], recv[k], NT).reshape(N, CAP, recv.shape[1])
                    for k in (2 * h, 2 * h + 1)
                ]
                cand[:, pair(h), :] = jnp.concatenate(tiles, axis=1).astype(BF16)
            return 0

        lax.fori_loop(0, N // 8, group, 0)

    def filtered(taps, before, seq):
        lane = iota(seq.shape, 1)
        feat = taps[0] * seq
        for i in (1, 2):
            moved = jnp.where(lane < i, pltpu.roll(before, i, 1), pltpu.roll(seq, i, 1))
            feat = feat + taps[i] * moved
        return feat

    spread(kv_recv, kv_sems, kv_cand)

    def block(o, before):
        seq = dot(kv_cand[o], place[o], TN)
        feat = filtered(kv_taps, before, seq)
        prod[pl.ds(pl.multiple_of(o * C, C), C), :] = feat[:C] * feat[C:]
        return seq

    lax.fori_loop(0, N, block, jnp.zeros((2 * C, B), F32), unroll=8)

    forward(prod, None, first_ref, tw_ref, fwd_ref, spec_p)

    spread(q_recv, q_sems, q_cand)

    def q_block(o, before):
        seq = dot(q_cand[o], place[o], TN)
        q_feat[pl.ds(pl.multiple_of(o * C, C), C), :] = filtered(q_taps, before, seq)
        return seq

    lax.fori_loop(0, N, q_block, jnp.zeros((C, B), F32), unroll=8)

    arrived(f_recv.at[pl.ds(0, (N - 1) * C)], recv_sems.at[2])
    filt[...] = f_recv[...].astype(jnp.int32).astype(F32)
    units = unit_of(jnp.floor(note_recv[:, 0, :] * (1.0 / LEVEL)))
    units = pltpu.roll(units, lax.rem(B - lax.rem(me, per) * C, B), 1)
    forward(filt, units, first_ref, tw_ref, fwd_ref, spec_f)

    a_re, a_im = spec_p[:, :B], spec_p[:, B:]
    b_re, b_im = spec_f[:, :B], spec_f[:, B:]
    z = jnp.concatenate([a_re * b_re - a_im * b_im, a_re * b_im + a_im * b_re], axis=1)
    spec_p[...] = wide(z, inv_ref)
    cos, sin = tw_ref[0], tw_ref[1]
    last = last_ref[...]
    for start in range(0, C, 2):
        group = range(start, start + 2)
        parts = []
        for c in group:
            y = spec_p[pl.ds(c * N, N), :]
            re, im = y[:, :B], y[:, B:]
            parts.append(jnp.concatenate([re * cos - im * sin, im * cos + re * sin], axis=0))
        hi, lo = halves(jnp.concatenate(parts, axis=1))
        y = dot(last, jnp.concatenate([hi, lo, hi], axis=0))
        for i, c in enumerate(group):
            conv[pl.ds(c, N, C), :] = y[:, i * B : (i + 1) * B]

    for start in range(0, N, 8):
        first_owner = partner(me, start) // 8 * 8
        plane = pl.ds(pl.multiple_of(first_owner * C, 8 * C), 8 * C)

        def blocks(ref):
            return ref[plane, :].reshape(8, C, B)

        gated = blocks(q_feat) * (blocks(conv) + gain[None] * blocks(prod))
        o_send[plane, :] = gated.astype(BF16).reshape(8 * C, B)
        lax.fori_loop(start, min(start + 8, N - 1), send_out, 0)
    out_ref[mine, :] = o_send[mine, :]

    most = pl.ds(0, (N - 1) * C)
    arrived(out_ref.at[most], recv_sems.at[4])
    arrived(note_recv.at[pl.ds(0, N - 1)], send_sems.at[0])
    arrived(kv_send.at[pl.ds(0, N - 1)], send_sems.at[1])
    arrived(f_send.at[most], send_sems.at[2])
    arrived(q_send.at[pl.ds(0, N - 1)], send_sems.at[3])
    arrived(o_send.at[most], send_sems.at[4])


def body(loader_rows, row_pos, short_w, long_filter, skip_gain):
    first, twiddle, fwd, inv, last = (jnp.asarray(t) for t in tables())
    operands = [
        row_pos.reshape(1, B), loader_rows, long_filter, short_w, skip_gain.reshape(1, W),
        first, twiddle, last, fwd, inv,
    ]
    turned = pl.pallas_call(
        kernel,
        out_shape=pltpu.VMEM((W, B), BF16),
        in_specs=[pl.BlockSpec(memory_space=pltpu.HBM)] * ARGS,
        out_specs=pl.BlockSpec(memory_space=pltpu.VMEM),
        scratch_shapes=[
            *(pltpu.VMEM(x.shape, x.dtype) for x in operands),
            pltpu.VMEM((N, 2 * C, B), BF16),
            pltpu.VMEM((N, C, B), BF16),
            pltpu.VMEM((W, B), jnp.int16),
            pltpu.VMEM((W // B, 1, B), F32),
            pltpu.VMEM((N, 2 * C, B), BF16),
            pltpu.VMEM((N, C, B), BF16),
            pltpu.VMEM((W, B), jnp.int16),
            pltpu.VMEM((N, 1, B), F32),
            pltpu.VMEM((N, N * CAP, B), BF16),
            pltpu.VMEM((N, N * CAP, B), BF16),
            pltpu.VMEM((N, N * CAP, 2 * C), BF16),
            pltpu.VMEM((N, N * CAP, C), BF16),
            pltpu.VMEM((W, B), F32),
            pltpu.VMEM((W, B), F32),
            pltpu.VMEM((W, B), F32),
            pltpu.VMEM((W, 2 * B), F32),
            pltpu.VMEM((W, 2 * B), F32),
            pltpu.VMEM((W, B), F32),
            pltpu.VMEM((W, B), BF16),
            pltpu.SemaphoreType.DMA((5,)),
            pltpu.SemaphoreType.DMA((5,)),
            pltpu.SemaphoreType.DMA((N,)),
            pltpu.SemaphoreType.DMA((N,)),
            pltpu.SemaphoreType.DMA((ARGS,)),
        ],
        compiler_params=pltpu.CompilerParams(
            collective_id=0, has_side_effects=True, vmem_limit_bytes=54 << 20
        ),
    )(*operands)
    return turned.T


def solution(mesh):
    return jax.shard_map(
        body,
        mesh=mesh,
        in_specs=(P("ctx", "chan"), P("ctx"), P(None, "chan"), P("ctx", "chan"), P("chan")),
        out_specs=P("ctx", "chan"),
        check_vma=False,
    )
```
